128 devices in a mesh: row: 16 (over z, x), col: 8 (over y, core).
Axes of the slice: x: 4, y: 4, z: 4, core: 2. Of those that a mesh axis runs over, the one named last changes fastest.
Arguments:
- tokens: bfloat16 [2048, 4096], P('row', 'col'), may hold values from -6 to 6
- cotangent: bfloat16 [2048, 4096], P('row', 'col'), may hold values from -6 to 6
- norm_gain: float32 [4096], P('col'), may hold values from 0.5 to 2
- gate_weight: bfloat16 [4096, 14336], P('col', 'row'), may hold values from -0.09375 to 0.09375
- up_weight: bfloat16 [4096, 14336], P('col', 'row'), may hold values from -0.09375 to 0.09375
- down_weight: bfloat16 [14336, 4096], P('row', 'col'), may hold values from -0.046875 to 0.046875
- gate_blocks: int32 [32, 112], P('col', 'row'), may hold values 0 or 1
- up_blocks: int32 [32, 112], P('col', 'row'), may hold values 0 or 1
- down_blocks: int32 [112, 32], P('row', 'col'), may hold values 0 or 1
Outputs:
- mixed: bfloat16 [2048, 4096], P('row', 'col')
- input_gradient: bfloat16 [2048, 4096], P('row', 'col')
- gate_gradient: bfloat16 [4096, 14336], P('col', 'row')
- up_gradient: bfloat16 [4096, 14336], P('col', 'row')
- down_gradient: bfloat16 [14336, 4096], P('row', 'col')
The draws below stay inside these ranges and needn't reach their ends.
Inputs may be any that keep to these rules, and one draw needn't show every extreme that they name: `gate_blocks`: 1 keeps a block of 128 x 128 weights, 0 prunes it. `up_blocks`: 1 keeps a block of 128 x 128 weights, 0 prunes it. `down_blocks`: 1 keeps a block of 128 x 128 weights, 0 prunes it.
All inputs are finite; a program needn't handle non-finite values.
Results may differ from the reference program's by a relative error of at most 0.013.
Values may be sent and summed in bfloat16 or wider, within the bound.
A program may use at most 128 MiB of HBM per device.

```python
import math
import jax
import jax.numpy as jnp
from jax import lax

D = 4096
FF = 14336
BLOCK = 128
TOKENS = 2048


def set_ends(drawn, own_key, least, high):
    spot = [jax.random.randint(jax.random.fold_in(own_key, axis), (), 0, length) for axis, length in enumerate(drawn.shape)]
    widest = drawn.shape.index(max(drawn.shape))
    next_to = spot[:widest] + [(spot[widest] + 1) % drawn.shape[widest]] + spot[widest + 1:]
    return drawn.at[tuple(spot)].set(least).at[tuple(next_to)].set(high)


def block_scale(own_key, dims, cuts, smallest, high):
    def one(dim, parts):
        steps = jax.random.uniform(jax.random.fold_in(jax.random.fold_in(own_key, 6), dim), (parts,), jnp.float32, smallest / len(cuts), high / len(cuts))
        return jnp.repeat(jnp.exp(steps), dims[dim] // parts).reshape((-1,) + (1,) * (len(dims) - dim - 1))

    loudness = one(*cuts[0])
    for cut in cuts[1:]:
        loudness = loudness * one(*cut)
    return loudness


def bell_draw(stream_key, extent, deviation, reach, split=(), dtype=jnp.bfloat16):
    result = jax.random.normal(stream_key, extent, jnp.float32) * deviation
    if len(split) > 0:
        result = block_scale(stream_key, extent, split, -0.22, 0.18) * result
    return jnp.clip(result, min=-reach, max=reach).astype(dtype)


def setup_inputs(seed: int = 0) -> dict:
    seeds = jax.random.split(jax.random.key(seed), 10)
    return {
        "tokens": bell_draw(seeds[0], (TOKENS, D), 1.0, 6.0, ((0, 16), (1, 8))),
        "cotangent": bell_draw(seeds[1], (TOKENS, D), 1.0, 6.0, ((0, 16), (1, 8))),
        "norm_gain": jnp.clip(jnp.exp(math.log(2.0) - 1.3862944 * jax.random.uniform(seeds[2], (D,), jnp.float32) ** block_scale(seeds[2], (D,), ((0, 8),), -0.2, 0.2)), 0.5, 2.0),
        "gate_weight": bell_draw(seeds[3], (D, FF), D ** -0.5, 0.09375, ((0, 8), (1, 16))),
        "up_weight": bell_draw(seeds[4], (D, FF), D ** -0.5, 0.09375, ((0, 8), (1, 16))),
        "down_weight": bell_draw(seeds[5], (FF, D), FF ** -0.5, 0.046875, ((0, 16), (1, 8))),
        "gate_blocks": set_ends((jax.random.randint(seeds[6], (D // BLOCK, FF // BLOCK), 0, 2) < 1).astype(jnp.int32), jax.random.fold_in(seeds[6], 1), 0, 1),
        "up_blocks": set_ends((jax.random.randint(seeds[7], (D // BLOCK, FF // BLOCK), 0, 2) < 1).astype(jnp.int32), jax.random.fold_in(seeds[7], 1), 0, 1),
        "down_blocks": set_ends((jax.random.randint(seeds[8], (FF // BLOCK, D // BLOCK), 0, 2) < 1).astype(jnp.int32), jax.random.fold_in(seeds[8], 1), 0, 1),
    }


epsilon = 1e-05

def expand(weight, mask):
    mask_rows, mask_cols = mask.shape
    height = weight.shape[0] // mask_rows
    breadth = weight.shape[1] // mask_cols
    expanded = jnp.broadcast_to(mask[:, None, :, None], (mask_rows, height, mask_cols, breadth))
    return expanded.reshape(weight.shape)

def reference(tokens, cotangent, norm_gain, gate_weight, up_weight, down_weight, gate_blocks, up_blocks, down_blocks):
    gate_keep = expand(gate_weight, gate_blocks)
    up_keep = expand(up_weight, up_blocks)
    down_keep = expand(down_weight, down_blocks)
    gate_masked = gate_weight * gate_keep.astype(jnp.bfloat16)
    up_masked = up_weight * up_keep.astype(jnp.bfloat16)
    down_masked = down_weight * down_keep.astype(jnp.bfloat16)
    width = tokens.shape[1]
    raw = tokens.astype(jnp.float32)
    scaled = (raw * norm_gain).astype(jnp.bfloat16)
    inv_rms = 1.0 / jnp.sqrt(lax.optimization_barrier(jnp.sum(raw * raw, axis=1)) / width + epsilon)
    pre_gate = jnp.dot(scaled, gate_masked, preferred_element_type=jnp.float32)
    pre_up = jnp.dot(scaled, up_masked, preferred_element_type=jnp.float32)
    factor = inv_rms[:, None]
    gate = factor * pre_gate
    up = factor * pre_up
    sigma = jax.nn.sigmoid(gate)
    activ = gate * sigma
    hidden = (activ * up).astype(jnp.bfloat16)
    mixed = (raw + jnp.dot(hidden, down_masked, preferred_element_type=jnp.float32)).astype(jnp.bfloat16)
    back_hidden = jnp.dot(cotangent, down_masked.T, preferred_element_type=jnp.float32)
    d_gate = back_hidden * up * sigma * (1.0 + gate * (1.0 - sigma))
    d_up = back_hidden * activ
    gate_pull = (factor * d_gate).astype(jnp.bfloat16)
    up_pull = (factor * d_up).astype(jnp.bfloat16)
    rms_pull = lax.optimization_barrier(jnp.sum(d_gate * pre_gate + d_up * pre_up, axis=1))
    scaled_pull = jnp.dot(gate_pull, gate_masked.T, preferred_element_type=jnp.float32) + jnp.dot(up_pull, up_masked.T, preferred_element_type=jnp.float32)
    correction = raw * (inv_rms * inv_rms * inv_rms * rms_pull / width)[:, None]
    input_gradient = (cotangent.astype(jnp.float32) + norm_gain * scaled_pull - correction).astype(jnp.bfloat16)
    gate_gradient = (gate_keep.astype(jnp.float32) * jnp.dot(scaled.T, gate_pull, preferred_element_type=jnp.float32)).astype(jnp.bfloat16)
    up_gradient = (up_keep.astype(jnp.float32) * jnp.dot(scaled.T, up_pull, preferred_element_type=jnp.float32)).astype(jnp.bfloat16)
    down_gradient = (down_keep.astype(jnp.float32) * jnp.dot(hidden.T, cotangent, preferred_element_type=jnp.float32)).astype(jnp.bfloat16)
    return (mixed, input_gradient, gate_gradient, up_gradient, down_gradient)
```

```python
import jax
import jax.numpy as jnp
from jax import lax
from jax.experimental import pallas as pl
from jax.experimental.pallas import tpu as pltpu
from jax.sharding import PartitionSpec as P

epsilon = 1e-05
MESH = pl.DeviceIdType.MESH
BF = jnp.bfloat16
F32 = jnp.float32

CHUNKS = 4
TOK = 16
HALF = 64
WIDE = 512
CHIP = 1024
FF = 896
GU = 2 * FF
ALL = 3 * FF
MODEL = 4096


def mm(a, b):
    return jnp.dot(a, b, preferred_element_type=F32)


def mm_nt(a, b):
    return lax.dot_general(a, b, (((1,), (1,)), ((), ())), preferred_element_type=F32)


def body(
    tok_ref, cot_ref, gain_ref, gw_ref, uw_ref, dw_ref, gm_ref, um_ref, dm_ref,
    mixed_ref, ig_ref, gg_ref, ug_ref, dg_ref,
    tokb, cotb, gain8, gainb, ssq, invb, rmsb, gath, wgu, wd, part, rel, full, hid, outp, rs1, sum1, rs2,
    fw, bw, acc_gu, acc_d, xt, ht, send_gu, send_d, recv_gu, recv_d, mixb, igb,
    sw_s, sw_r, sq_s, sq_r, p1_s, p1_r, p2_s, p2_r, r_s, r_r, f_s, f_r, g_s, g_r, h_s, h_r,
    a_s, a_r, b_s, b_r, w_s, w_r, m_s, m_r, o_s, o_r,
):
    row = lax.axis_index("row")
    col = lax.axis_index("col")
    z, x, y, c = row // 4, row % 4, col // 2, col % 2
    other = 1 - c
    up, dn, op = (y + 1) % 4, (y + 3) % 4, (y + 2) % 4

    def dev(dz, dx, dy, dc):
        return (dz * 4 + dx, dy * 2 + dc)

    twin = dev(z, x, y, other)
    up_dev, dn_dev = dev(z, x, up, c), dev(z, x, dn, c)

    def zdev(j):
        return dev((z + j) % 4, x, y, c)

    def xdev(j):
        return dev(z, (x + j) % 4, y, c)

    def ydev(j):
        return dev(z, x, (y + j) % 4, c)

    def rc(src, dst, ss, rs, to):
        return pltpu.make_async_remote_copy(
            src_ref=src, dst_ref=dst, send_sem=ss, recv_sem=rs, device_id=to, device_id_type=MESH
        )

    def start(copies):
        for copy in copies:
            copy.start()

    def finish(copies):
        for copy in copies:
            copy.wait()

    lo = pl.ds(0, CHIP)
    hi = pl.ds(CHIP, CHIP)
    mine = pl.ds(pl.multiple_of(c * WIDE, WIDE), WIDE)
    theirs = pl.ds(pl.multiple_of(other * WIDE, WIDE), WIDE)
    my_rows = pl.ds(pl.multiple_of(c * HALF, HALF), HALF)
    their_rows = pl.ds(pl.multiple_of(other * HALF, HALF), HALF)

    barrier = pltpu.get_barrier_semaphore()
    peers = [twin] + [f(j) for f in (xdev, ydev, zdev) for j in (1, 2, 3)]
    for peer in peers:
        pl.semaphore_signal(barrier, inc=1, device_id=peer, device_id_type=MESH)

    @pl.loop(0, 4)
    def _(i):
        rows = pl.ds(pl.multiple_of(i * 128, 128), 128)
        to = pl.ds(pl.multiple_of(c * WIDE + i * 128, 128), 128)
        for j in range(7):
            cols = slice(j * 128, j * 128 + 128)
            keep = gm_ref[i, j].astype(F32)
            wgu[to, j * 128 : j * 128 + 128] = (gw_ref[rows, cols].astype(F32) * keep).astype(BF)
            keep = um_ref[i, j].astype(F32)
            wgu[to, FF + j * 128 : FF + j * 128 + 128] = (uw_ref[rows, cols].astype(F32) * keep).astype(BF)

    @pl.loop(0, 7)
    def _(i):
        rows = pl.ds(pl.multiple_of(i * 128, 128), 128)
        for j in range(4):
            to = pl.ds(pl.multiple_of(c * WIDE + j * 128, 128), 128)
            keep = dm_ref[i, j].astype(F32)
            wd[rows, to] = (dw_ref[rows, j * 128 : j * 128 + 128].astype(F32) * keep).astype(BF)

    gain8[...] = jnp.broadcast_to(gain_ref[...], (8, WIDE))
    tokb[:, mine] = tok_ref[my_rows, :]
    cotb[:, mine] = cot_ref[my_rows, :]
    gainb[:, mine] = gain8[...]

    pl.semaphore_wait(barrier, len(peers))

    swaps = [
        rc(cot_ref.at[their_rows, :], cotb.at[:, mine], sw_s.at[0], sw_r.at[0], twin),
        rc(tok_ref.at[their_rows, :], tokb.at[:, mine], sw_s.at[1], sw_r.at[1], twin),
        rc(gain8, gainb.at[:, mine], sw_s.at[2], sw_r.at[2], twin),
        rc(wd.at[:, mine], wd.at[:, mine], sw_s.at[3], sw_r.at[3], twin),
        rc(wgu.at[mine, :], wgu.at[mine, :], sw_s.at[4], sw_r.at[4], twin),
    ]
    start(swaps)

    def gather_x(k):
        return [
            rc(gath.at[k, z, x, :, lo], gath.at[k, z, x, :, lo], p1_s.at[k, 0, j - 1], p1_r.at[k, 0, j - 1], xdev(j))
            for j in (1, 2, 3)
        ]

    def gather_z(k):
        return [
            rc(gath.at[k, z, x, :, hi], gath.at[k, z, x, :, hi], p1_s.at[k, 1, j - 1], p1_r.at[k, 1, j - 1], zdev(j))
            for j in (1, 2, 3)
        ]

    def gather_rest(k):
        return [
            rc(gath.at[k, z, :, :, lo], gath.at[k, z, :, :, lo], p2_s.at[k, 0, j - 1], p2_r.at[k, 0, j - 1], zdev(j))
            for j in (1, 2, 3)
        ] + [
            rc(gath.at[k, :, x, :, hi], gath.at[k, :, x, :, hi], p2_s.at[k, 1, j - 1], p2_r.at[k, 1, j - 1], xdev(j))
            for j in (1, 2, 3)
        ]

    finish(swaps[0:1])
    for k in range(CHUNKS):
        gath[k, z, x, :, hi] = cotb[k * TOK : (k + 1) * TOK, :]
    start(gather_z(0))

    finish(swaps[1:3])
    tok = tokb[...].astype(F32)
    ssq[y] = jnp.broadcast_to(jnp.sum(tok * tok, axis=1, keepdims=True), (HALF, 128))
    sends = [rc(ssq.at[y], ssq.at[y], sq_s.at[j - 1], sq_r.at[j - 1], ydev(j)) for j in (1, 2, 3)]
    start(sends)
    finish(sends)
    invb[...] = 1.0 / jnp.sqrt((ssq[0] + ssq[1] + ssq[2] + ssq[3]) / MODEL + epsilon)
    for k in range(CHUNKS):
        rows = slice(k * TOK, (k + 1) * TOK)
        scaled = tokb[rows, :].astype(F32) * gainb[0:1, :] * invb[rows, 0:1]
        gath[k, z, x, :, lo] = scaled.astype(BF)
    start(gather_x(0))

    @pl.loop(0, 16)
    def _(i):
        acc_gu[pl.ds(pl.multiple_of(i * 64, 64), 64), :] = jnp.zeros((64, GU), F32)
        acc_d[pl.ds(pl.multiple_of(i * 56, 56), 56), :] = jnp.zeros((56, CHIP), F32)

    finish(gather_z(0))
    finish(gather_x(0))
    start(gather_rest(0))
    start(gather_x(1) + gather_z(1))
    finish(swaps[3:5])

    def relay(k, s):
        return [
            rc(part.at[s, op, pl.ds(0, 32), :], rel.at[k, 0], r_s.at[k, 0], r_r.at[k, 0], up_dev),
            rc(part.at[s, op, pl.ds(32, 32), :], rel.at[k, 1], r_s.at[k, 1], r_r.at[k, 1], dn_dev),
        ]

    def quarter(k, s):
        return [
            rc(part.at[s, up], full.at[k, 0], f_s.at[k, 0], f_r.at[k, 0], up_dev),
            rc(part.at[s, dn], full.at[k, 1], f_s.at[k, 1], f_r.at[k, 1], dn_dev),
        ]

    def share(k):
        return [
            rc(hid.at[k, y], hid.at[k, y], g_s.at[k, 0], g_r.at[k, 0], up_dev),
            rc(hid.at[k, y], hid.at[k, y], g_s.at[k, 1], g_r.at[k, 1], dn_dev),
        ]

    def pass_on(k):
        first = hid.at[k, dn, pl.ds(0, 32), :]
        second = hid.at[k, up, pl.ds(32, 32), :]
        return [
            rc(first, first, h_s.at[k, 0], h_r.at[k, 0], up_dev),
            rc(second, second, h_s.at[k, 1], h_r.at[k, 1], dn_dev),
        ]

    def scatter(k, s):
        return [
            rc(outp.at[s, :, (x + j) % 4, :, lo], rs1.at[k, 0, j - 1], a_s.at[k, 0, j - 1], a_r.at[k, 0, j - 1], xdev(j))
            for j in (1, 2, 3)
        ] + [
            rc(outp.at[s, (z + j) % 4, :, :, hi], rs1.at[k, 1, j - 1], a_s.at[k, 1, j - 1], a_r.at[k, 1, j - 1], zdev(j))
            for j in (1, 2, 3)
        ]

    def scatter_rest(k):
        return [
            rc(sum1.at[k, 0, (z + j) % 4], rs2.at[k, 0, j - 1], b_s.at[k, 0, j - 1], b_r.at[k, 0, j - 1], zdev(j))
            for j in (1, 2, 3)
        ] + [
            rc(sum1.at[k, 1, (x + j) % 4], rs2.at[k, 1, j - 1], b_s.at[k, 1, j - 1], b_r.at[k, 1, j - 1], xdev(j))
            for j in (1, 2, 3)
        ]

    def project(k):
        s = k % 2

        @pl.loop(0, 7)
        def _(n):
            cols = pl.ds(pl.multiple_of(n * 256, 256), 256)
            got = mm(gath[k, :, :, :, lo].reshape(256, CHIP), wgu[:, cols])
            part[s, :, :, cols] = got.astype(BF).reshape(4, 64, 256)

        for n, wide in ((0, 256), (256, 256), (512, 256), (768, 128)):
            got = mm_nt(gath[k, :, :, :, hi].reshape(256, CHIP), wd[n : n + wide, :])
            part[s, :, :, GU + n : GU + n + wide] = got.astype(BF).reshape(4, 64, wide)

    def add_relay(k):
        s = k % 2

        @pl.loop(0, 7)
        def _(n):
            cols = pl.ds(pl.multiple_of(n * 384, 128), 384)
            part[s, up, 0:32, cols] = (part[s, up, 0:32, cols].astype(F32) + rel[k, 0, :, cols].astype(F32)).astype(BF)
            part[s, dn, 32:64, cols] = (part[s, dn, 32:64, cols].astype(F32) + rel[k, 1, :, cols].astype(F32)).astype(BF)

    def activate(k):
        s = k % 2

        @pl.loop(0, 7)
        def _(n):
            def total(base):
                cols = pl.ds(pl.multiple_of(base + n * 128, 128), 128)
                return part[s, y, :, cols].astype(F32) + full[k, 0, :, cols].astype(F32) + full[k, 1, :, cols].astype(F32)

            gate, up_value, back = total(0), total(FF), total(GU)
            sigma = jax.nn.sigmoid(gate)
            activ = gate * sigma
            d_gate = back * up_value * sigma * (1.0 + gate * (1.0 - sigma))
            hid[k, y, :, pl.ds(pl.multiple_of(n * 128, 128), 128)] = (activ * up_value).astype(BF)
            hid[k, y, :, pl.ds(pl.multiple_of(FF + n * 128, 128), 128)] = d_gate.astype(BF)
            hid[k, y, :, pl.ds(pl.multiple_of(GU + n * 128, 128), 128)] = (back * activ).astype(BF)

    def products(k):
        s = k % 2

        @pl.loop(0, 4)
        def _(n):
            cols = pl.ds(pl.multiple_of(n * 256, 256), 256)
            got = mm(hid[k, :, :, 0:FF].reshape(256, FF), wd[:, cols])
            outp[s, :, :, :, cols] = got.astype(BF).reshape(4, 4, TOK, 256)
            got = mm_nt(hid[k, :, :, FF:ALL].reshape(256, GU), wgu[cols, :])
            outp[s, :, :, :, pl.ds(pl.multiple_of(CHIP + n * 256, 256), 256)] = got.astype(BF).reshape(4, 4, TOK, 256)

    def weight_sums(k):
        xt[...] = gath[k, :, :, :, lo].reshape(256, CHIP).T
        ht[...] = hid[k, :, :, 0:FF].reshape(256, FF).T

        @pl.loop(0, 7)
        def _(n):
            cols = pl.ds(pl.multiple_of(n * 256, 256), 256)
            from_cols = pl.ds(pl.multiple_of(FF + n * 256, 128), 256)
            pulled = hid[k, :, :, from_cols].reshape(256, 256)
            for m in range(4):
                acc_gu[m * 256 : m * 256 + 256, cols] += mm(xt[m * 256 : m * 256 + 256, :], pulled)

        @pl.loop(0, 4)
        def _(n):
            cols = pl.ds(pl.multiple_of(n * 256, 256), 256)
            from_cols = pl.ds(pl.multiple_of(CHIP + n * 256, 256), 256)
            cots = gath[k, :, :, :, from_cols].reshape(256, 256)
            for m, high in ((0, 256), (256, 256), (512, 256), (768, 128)):
                acc_d[m : m + high, cols] += mm(ht[m : m + high, :], cots)

    def sum_first(k):
        s = k % 2
        for i in range(4):
            total = outp[s, i, x, :, lo].astype(F32)
            for j in range(3):
                total += rs1[k, 0, j, i].astype(F32)
            sum1[k, 0, i] = total.astype(BF)
            total = outp[s, z, i, :, hi].astype(F32)
            for j in range(3):
                total += rs1[k, 1, j, i].astype(F32)
            sum1[k, 1, i] = total.astype(BF)

    def sum_last(k):
        rows = pl.ds(pl.multiple_of(k * TOK, TOK), TOK)
        total = sum1[k, 0, z].astype(F32)
        for j in range(3):
            total += rs2[k, 0, j].astype(F32)
        fw[rows, :] = total
        total = sum1[k, 1, x].astype(F32)
        for j in range(3):
            total += rs2[k, 1, j].astype(F32)
        bw[rows, :] = total

    exchange = [
        rc(send_gu, recv_gu, w_s.at[0], w_r.at[0], twin),
        rc(send_d, recv_d, w_s.at[1], w_r.at[1], twin),
    ]

    def step(i, carry):
        def at(k):
            return jnp.logical_and(k >= 0, k < CHUNKS)

        @pl.when(at(i - 2))
        def _():
            k = i - 2
            finish(quarter(k, k % 2))
            activate(k)
            start(share(k))

        @pl.when(at(i - 1))
        def _():
            k = i - 1
            finish(relay(k, k % 2))
            add_relay(k)
            start(quarter(k, k % 2))

        @pl.when(i + 1 < CHUNKS)
        def _():
            finish(gather_x(i + 1) + gather_z(i + 1))
            start(gather_rest(i + 1))

        @pl.when(i + 2 < CHUNKS)
        def _():
            start(gather_x(i + 2) + gather_z(i + 2))

        @pl.when(i < CHUNKS)
        def _():
            finish(gather_rest(i))
            project(i)
            start(relay(i, i % 2))

        @pl.when(at(i - 4))
        def _():
            k = i - 4
            finish(scatter(k, k % 2))
            sum_first(k)
            start(scatter_rest(k))

        @pl.when(at(i - 3))
        def _():
            k = i - 3
            finish(pass_on(k))
            products(k)
            start(scatter(k, k % 2))
            weight_sums(k)

        @pl.when(i - 3 == CHUNKS - 1)
        def _():
            @pl.loop(0, 4)
            def _(n):
                rows = pl.ds(pl.multiple_of(n * 128, 128), 128)
                src = pl.ds(pl.multiple_of(other * WIDE + n * 128, 128), 128)
                send_gu[rows, :] = acc_gu[src, :].astype(BF)

            send_d[...] = acc_d[:, theirs].astype(BF)
            start(exchange)

        @pl.when(at(i - 5))
        def _():
            k = i - 5
            finish(scatter_rest(k))
            sum_last(k)

        @pl.when(at(i - 2))
        def _():
            k = i - 2
            finish(share(k))
            start(pass_on(k))

        return carry

    lax.fori_loop(0, CHUNKS + 5, step, 0)

    pull = jnp.sum(tokb[...].astype(F32) * gainb[0:1, :] * bw[...], axis=1, keepdims=True)
    rmsb[y] = jnp.broadcast_to(pull, (HALF, 128)) * invb[...]
    sends = [rc(rmsb.at[y], rmsb.at[y], m_s.at[j - 1], m_r.at[j - 1], ydev(j)) for j in (1, 2, 3)]
    start(sends)
    mixb[...] = (tokb[...].astype(F32) + fw[...]).astype(BF)
    mixed_ref[my_rows, :] = mixb[:, mine]
    back = [rc(mixb.at[:, theirs], mixed_ref.at[my_rows, :], o_s.at[0], o_r.at[0], twin)]
    start(back)
    finish(sends)
    inv = invb[:, 0:1]
    fix = inv * inv * ((rmsb[0] + rmsb[1]) + (rmsb[2] + rmsb[3]))[:, 0:1] / MODEL
    igb[...] = (
        cotb[...].astype(F32) + gainb[0:1, :] * (inv * bw[...]) - tokb[...].astype(F32) * fix
    ).astype(BF)
    ig_ref[my_rows, :] = igb[:, mine]
    back += [rc(igb.at[:, theirs], ig_ref.at[my_rows, :], o_s.at[1], o_r.at[1], twin)]
    start(back[1:])

    finish(exchange)

    @pl.loop(0, 4)
    def _(i):
        rows = pl.ds(pl.multiple_of(i * 128, 128), 128)
        src = pl.ds(pl.multiple_of(c * WIDE + i * 128, 128), 128)
        for j in range(7):
            cols = slice(j * 128, j * 128 + 128)
            wide = slice(FF + j * 128, FF + j * 128 + 128)
            total = acc_gu[src, cols] + recv_gu[rows, cols].astype(F32)
            gg_ref[rows, cols] = (total * gm_ref[i, j].astype(F32)).astype(BF)
            total = acc_gu[src, wide] + recv_gu[rows, wide].astype(F32)
            ug_ref[rows, cols] = (total * um_ref[i, j].astype(F32)).astype(BF)

    @pl.loop(0, 7)
    def _(i):
        rows = pl.ds(pl.multiple_of(i * 128, 128), 128)
        for j in range(4):
            cols = slice(j * 128, j * 128 + 128)
            src = pl.ds(pl.multiple_of(c * WIDE + j * 128, 128), 128)
            total = acc_d[rows, src] + recv_d[rows, cols].astype(F32)
            dg_ref[rows, cols] = (total * dm_ref[i, j].astype(F32)).astype(BF)

    finish(back)


def shards(tokens, cotangent, norm_gain, gate_w, up_w, down_w, gate_b, up_b, down_b):
    vmem = pl.BlockSpec(memory_space=pltpu.VMEM)
    smem = pl.BlockSpec(memory_space=pltpu.SMEM)

    def dma(*shape):
        return [pltpu.SemaphoreType.DMA(shape)] * 2

    V = pltpu.VMEM
    out = jax.ShapeDtypeStruct
    return pl.pallas_call(
        body,
        out_shape=(
            out(tokens.shape, BF),
            out(tokens.shape, BF),
            out(gate_w.shape, BF),
            out(up_w.shape, BF),
            out(down_w.shape, BF),
        ),
        in_specs=[vmem] * 6 + [smem] * 3,
        out_specs=(vmem,) * 5,
        scratch_shapes=[
            V((HALF, CHIP), BF),
            V((HALF, CHIP), BF),
            V((8, WIDE), F32),
            V((8, CHIP), F32),
            V((4, HALF, 128), F32),
            V((HALF, 128), F32),
            V((4, HALF, 128), F32),
            V((CHUNKS, 4, 4, TOK, 2 * CHIP), BF),
            V((CHIP, GU), BF),
            V((FF, CHIP), BF),
            V((2, 4, 64, ALL), BF),
            V((CHUNKS, 2, 32, ALL), BF),
            V((CHUNKS, 2, 64, ALL), BF),
            V((CHUNKS, 4, 64, ALL), BF),
            V((2, 4, 4, TOK, 2 * CHIP), BF),
            V((CHUNKS, 2, 3, 4, TOK, CHIP), BF),
            V((CHUNKS, 2, 4, TOK, CHIP), BF),
            V((CHUNKS, 2, 3, TOK, CHIP), BF),
            V((HALF, CHIP), F32),
            V((HALF, CHIP), F32),
            V((CHIP, GU), F32),
            V((FF, CHIP), F32),
            V((CHIP, 256), BF),
            V((FF, 256), BF),
            V((WIDE, GU), BF),
            V((FF, WIDE), BF),
            V((WIDE, GU), BF),
            V((FF, WIDE), BF),
            V((HALF, CHIP), BF),
            V((HALF, CHIP), BF),
        ]
        + dma(5)
        + dma(3)
        + dma(CHUNKS, 2, 3)
        + dma(CHUNKS, 2, 3)
        + dma(CHUNKS, 2)
        + dma(CHUNKS, 2)
        + dma(CHUNKS, 2)
        + dma(CHUNKS, 2)
        + dma(CHUNKS, 2, 3)
        + dma(CHUNKS, 2, 3)
        + dma(2)
        + dma(3)
        + dma(2),
        compiler_params=pltpu.CompilerParams(
            collective_id=0, has_side_effects=True, vmem_limit_bytes=62 * 1024 * 1024
        ),
        cost_estimate=pl.CostEstimate(flops=17_000_000_000, bytes_accessed=6_000_000, transcendentals=2_000_000),
        name="ffn",
    )(tokens, cotangent, norm_gain.reshape(1, -1), gate_w, up_w, down_w, gate_b, up_b, down_b)


def solution(mesh):
    in_specs = (
        P("row", "col"),
        P("row", "col"),
        P("col"),
        P("col", "row"),
        P("col", "row"),
        P("row", "col"),
        P("col", "row"),
        P("col", "row"),
        P("row", "col"),
    )
    out_specs = (
        P("row", "col"),
        P("row", "col"),
        P("col", "row"),
        P("col", "row"),
        P("row", "col"),
    )
    return jax.shard_map(shards, mesh=mesh, in_specs=in_specs, out_specs=out_specs, check_vma=False)
```

```python
import jax
import jax.numpy as jnp
from jax import lax
from jax.experimental import pallas as pl
from jax.experimental.pallas import tpu as pltpu
from jax.sharding import PartitionSpec as P

epsilon = 1e-05
MESH = pl.DeviceIdType.MESH
BF = jnp.bfloat16
F32 = jnp.float32

CHUNKS = 4
TOK = 16
HALF = 64
WIDE = 512
CHIP = 1024
FF = 896
GU = 2 * FF
ALL = 3 * FF
MODEL = 4096


def mm(a, b):
    return jnp.dot(a, b, preferred_element_type=F32)


def mm_nt(a, b):
    return lax.dot_general(a, b, (((1,), (1,)), ((), ())), preferred_element_type=F32)


def body(
    tok_ref, cot_ref, gain_ref, gw_ref, uw_ref, dw_ref, gm_ref, um_ref, dm_ref,
    mixed_ref, ig_ref, gg_ref, ug_ref, dg_ref,
    tokb, cotb, gain8, gainb, ssq, invb, rmsb, gath, wgu, wd, part, rel, full, hid, outp, rs1, sum1, rs2,
    fw, bw, acc_gu, acc_d, xt, ht, send_gu, send_d, recv_gu, recv_d, mixb, igb,
    sw_s, sw_r, sq_s, sq_r, p1_s, p1_r, p2_s, p2_r, r_s, r_r, f_s, f_r, g_s, g_r, h_s, h_r,
    a_s, a_r, b_s, b_r, w_s, w_r, m_s, m_r, o_s, o_r,
):
    row = lax.axis_index("row")
    col = lax.axis_index("col")
    z, x, y, c = row // 4, row % 4, col // 2, col % 2
    other = 1 - c
    up, dn, op = (y + 1) % 4, (y + 3) % 4, (y + 2) % 4

    def dev(dz, dx, dy, dc):
        return (dz * 4 + dx, dy * 2 + dc)

    twin = dev(z, x, y, other)
    up_dev, dn_dev = dev(z, x, up, c), dev(z, x, dn, c)

    def zdev(j):
        return dev((z + j) % 4, x, y, c)

    def xdev(j):
        return dev(z, (x + j) % 4, y, c)

    def ydev(j):
        return dev(z, x, (y + j) % 4, c)

    def rc(src, dst, ss, rs, to):
        return pltpu.make_async_remote_copy(
            src_ref=src, dst_ref=dst, send_sem=ss, recv_sem=rs, device_id=to, device_id_type=MESH
        )

    def start(copies):
        for copy in copies:
            copy.start()

    def finish(copies):
        for copy in copies:
            copy.wait()

    lo = pl.ds(0, CHIP)
    hi = pl.ds(CHIP, CHIP)

    def strip(a, h):
        return pl.ds(a * CHIP + h * WIDE, WIDE)

    spot = lax.broadcasted_iota(jnp.int32, (HALF, 128), 0) == lax.broadcasted_iota(jnp.int32, (HALF, 128), 1)

    def to_lanes(column):
        line = jnp.sum(jnp.where(spot, jnp.broadcast_to(column, (HALF, 128)), 0.0), axis=0, keepdims=True)
        return jnp.broadcast_to(line, (8, 128))

    def to_column(line):
        return jnp.sum(jnp.where(spot, jnp.broadcast_to(line, (HALF, 128)), 0.0), axis=1, keepdims=True)

    mine = pl.ds(pl.multiple_of(c * WIDE, WIDE), WIDE)
    theirs = pl.ds(pl.multiple_of(other * WIDE, WIDE), WIDE)
    my_rows = pl.ds(pl.multiple_of(c * HALF, HALF), HALF)
    their_rows = pl.ds(pl.multiple_of(other * HALF, HALF), HALF)

    barrier = pltpu.get_barrier_semaphore()
    peers = [twin] + [f(j) for f in (xdev, ydev, zdev) for j in (1, 2, 3)]
    for peer in peers:
        pl.semaphore_signal(barrier, inc=1, device_id=peer, device_id_type=MESH)

    @pl.loop(0, 4)
    def _(i):
        rows = pl.ds(pl.multiple_of(i * 128, 128), 128)
        to = pl.ds(pl.multiple_of(c * WIDE + i * 128, 128), 128)
        for j in range(7):
            cols = slice(j * 128, j * 128 + 128)
            keep = gm_ref[i, j].astype(F32)
            wgu[to, j * 128 : j * 128 + 128] = (gw_ref[rows, cols].astype(F32) * keep).astype(BF)
            keep = um_ref[i, j].astype(F32)
            wgu[to, FF + j * 128 : FF + j * 128 + 128] = (uw_ref[rows, cols].astype(F32) * keep).astype(BF)

    @pl.loop(0, 7)
    def _(i):
        rows = pl.ds(pl.multiple_of(i * 128, 128), 128)
        for j in range(4):
            to = pl.ds(pl.multiple_of(c * WIDE + j * 128, 128), 128)
            keep = dm_ref[j, i].astype(F32)
            wd[rows, to] = (dw_ref[rows, j * 128 : j * 128 + 128].astype(F32) * keep).astype(BF)

    gain8[...] = jnp.broadcast_to(gain_ref[...], (8, WIDE))
    tokb[:, mine] = tok_ref[my_rows, :]
    cotb[:, mine] = cot_ref[my_rows, :]
    gainb[:, mine] = gain8[...]

    pl.semaphore_wait(barrier, len(peers))

    swaps = [
        rc(cot_ref.at[their_rows, :], cotb.at[:, mine], sw_s.at[0], sw_r.at[0], twin),
        rc(tok_ref.at[their_rows, :], tokb.at[:, mine], sw_s.at[1], sw_r.at[1], twin),
        rc(gain8, gainb.at[:, mine], sw_s.at[2], sw_r.at[2], twin),
        rc(wd.at[:, mine], wd.at[:, mine], sw_s.at[3], sw_r.at[3], twin),
        rc(wgu.at[mine, :], wgu.at[mine, :], sw_s.at[4], sw_r.at[4], twin),
    ]
    start(swaps)

    def near(k, a):
        def one(h, to, j):
            block = gath.at[k, z, x, :, strip(a, h)]
            return rc(block, block, p1_s.at[k, a, h, j - 1], p1_r.at[k, a, h, j - 1], to(j))

        return [one(h, to, j) for j in (1, 2, 3) for h, to in ((0, xdev), (1, zdev))]

    def rest(k, a):
        def one(h, to, j):
            block = gath.at[k, z, :, :, strip(a, 0)] if h == 0 else gath.at[k, :, x, :, strip(a, 1)]
            return rc(block, block, p2_s.at[k, a, h, j - 1], p2_r.at[k, a, h, j - 1], to(j))

        return [one(h, to, j) for j in (1, 2, 3) for h, to in ((0, zdev), (1, xdev))]

    finish(swaps[0:1])
    for k in range(CHUNKS):
        gath[k, z, x, :, hi] = cotb[k * TOK : (k + 1) * TOK, :]
    start(near(0, 1))

    finish(swaps[1:3])
    tok = tokb[...].astype(F32)
    ssq[y] = to_lanes(jnp.sum(tok * tok, axis=1, keepdims=True))
    sends = [rc(ssq.at[y], ssq.at[y], sq_s.at[j - 1], sq_r.at[j - 1], ydev(j)) for j in (1, 2, 3)]
    start(sends)
    finish(near(0, 1))
    start(rest(0, 1))
    finish(sends)
    squares = to_column(((ssq[0] + ssq[1]) + (ssq[2] + ssq[3]))[0:1, :])
    invb[...] = jnp.broadcast_to(1.0 / jnp.sqrt(squares / MODEL + epsilon), (HALF, 128))
    for k in range(CHUNKS):
        rows = slice(k * TOK, (k + 1) * TOK)
        scaled = tokb[rows, :].astype(F32) * gainb[0:1, :] * invb[rows, 0:1]
        gath[k, z, x, :, lo] = scaled.astype(BF)
    start(near(0, 0))

    @pl.loop(0, 16)
    def _(i):
        acc_gu[pl.ds(pl.multiple_of(i * 64, 64), 64), :] = jnp.zeros((64, GU), F32)
        acc_d[pl.ds(pl.multiple_of(i * 56, 56), 56), :] = jnp.zeros((56, CHIP), F32)

    finish(near(0, 0))
    start(rest(0, 0))
    start(near(1, 1) + near(1, 0))
    finish(swaps[3:5])

    def span(a):
        return pl.ds(GU, FF) if a == 1 else pl.ds(0, GU)

    def relay(k, s, a):
        one = part.at[s, op, pl.ds(0, 32), span(a)]
        two = part.at[s, op, pl.ds(32, 32), span(a)]
        return [
            rc(one, rel.at[k, 0, :, span(a)], r_s.at[k, a, 0], r_r.at[k, a, 0], up_dev),
            rc(two, rel.at[k, 1, :, span(a)], r_s.at[k, a, 1], r_r.at[k, a, 1], dn_dev),
        ]

    def quarter(k, s, a):
        return [
            rc(part.at[s, up, :, span(a)], full.at[k, 0, :, span(a)], f_s.at[k, a, 0], f_r.at[k, a, 0], up_dev),
            rc(part.at[s, dn, :, span(a)], full.at[k, 1, :, span(a)], f_s.at[k, a, 1], f_r.at[k, a, 1], dn_dev),
        ]

    def share(k, later):
        one = hid.at[k, y, pl.ds(32 if later else 0, 32), :]
        two = hid.at[k, y, pl.ds(0 if later else 32, 32), :]
        return [
            rc(one, one, g_s.at[k, later, 0], g_r.at[k, later, 0], up_dev),
            rc(two, two, g_s.at[k, later, 1], g_r.at[k, later, 1], dn_dev),
        ]

    def pass_on(k):
        first = hid.at[k, dn, pl.ds(0, 32), :]
        second = hid.at[k, up, pl.ds(32, 32), :]
        return [
            rc(first, first, h_s.at[k, 0], h_r.at[k, 0], up_dev),
            rc(second, second, h_s.at[k, 1], h_r.at[k, 1], dn_dev),
        ]

    def scatter(k, s, a):
        def one(h, to, j):
            block = outp.at[s, :, (x + j) % 4, :, strip(a, 0)] if h == 0 else outp.at[s, (z + j) % 4, :, :, strip(a, 1)]
            return rc(block, rs1.at[k, a, h, j - 1], a_s.at[k, a, h, j - 1], a_r.at[k, a, h, j - 1], to(j))

        return [one(h, to, j) for j in (1, 2, 3) for h, to in ((0, xdev), (1, zdev))]

    def scatter_rest(k, a):
        def one(h, to, j):
            block = sum1.at[k, a, h, ((z if h == 0 else x) + j) % 4]
            return rc(block, rs2.at[k, a, h, j - 1], b_s.at[k, a, h, j - 1], b_r.at[k, a, h, j - 1], to(j))

        return [one(h, to, j) for j in (1, 2, 3) for h, to in ((0, zdev), (1, xdev))]

    def project_pre(k):
        s = k % 2

        @pl.loop(0, 7)
        def _(n):
            cols = pl.ds(pl.multiple_of(n * 256, 256), 256)
            got = mm(gath[k, :, :, :, lo].reshape(256, CHIP), wgu[:, cols])
            part[s, :, :, cols] = got.astype(BF).reshape(4, 64, 256)

    def project_back(k):
        s = k % 2
        for n, wide in ((0, 256), (256, 256), (512, 256), (768, 128)):
            got = mm_nt(gath[k, :, :, :, hi].reshape(256, CHIP), wd[n : n + wide, :])
            part[s, :, :, GU + n : GU + n + wide] = got.astype(BF).reshape(4, 64, wide)

    def add_relay(k, a):
        s = k % 2
        base, count = (GU, 7) if a == 1 else (0, 14)

        @pl.loop(0, count)
        def _(n):
            cols = pl.ds(pl.multiple_of(base + n * 128, 128), 128)
            part[s, up, 0:32, cols] = (part[s, up, 0:32, cols].astype(F32) + rel[k, 0, :, cols].astype(F32)).astype(BF)
            part[s, dn, 32:64, cols] = (part[s, dn, 32:64, cols].astype(F32) + rel[k, 1, :, cols].astype(F32)).astype(BF)

    def activate(k):
        s = k % 2

        @pl.loop(0, 7)
        def _(n):
            def total(base):
                cols = pl.ds(pl.multiple_of(base + n * 128, 128), 128)
                return part[s, y, :, cols].astype(F32) + full[k, 0, :, cols].astype(F32) + full[k, 1, :, cols].astype(F32)

            gate, up_value, back = total(0), total(FF), total(GU)
            sigma = jax.nn.sigmoid(gate)
            activ = gate * sigma
            d_gate = back * up_value * sigma * (1.0 + gate * (1.0 - sigma))
            hid[k, y, :, pl.ds(pl.multiple_of(n * 128, 128), 128)] = (activ * up_value).astype(BF)
            hid[k, y, :, pl.ds(pl.multiple_of(FF + n * 128, 128), 128)] = d_gate.astype(BF)
            hid[k, y, :, pl.ds(pl.multiple_of(GU + n * 128, 128), 128)] = (back * activ).astype(BF)

    def products_back(k):
        s = k % 2

        @pl.loop(0, 4)
        def _(n):
            cols = pl.ds(pl.multiple_of(n * 256, 256), 256)
            got = mm_nt(hid[k, :, :, FF:ALL].reshape(256, GU), wgu[cols, :])
            outp[s, :, :, :, pl.ds(pl.multiple_of(CHIP + n * 256, 256), 256)] = got.astype(BF).reshape(4, 4, TOK, 256)

    def products_out(k):
        s = k % 2

        @pl.loop(0, 4)
        def _(n):
            cols = pl.ds(pl.multiple_of(n * 256, 256), 256)
            got = mm(hid[k, :, :, 0:FF].reshape(256, FF), wd[:, cols])
            outp[s, :, :, :, cols] = got.astype(BF).reshape(4, 4, TOK, 256)

    def weight_sums(k):
        xt[...] = gath[k, :, :, :, lo].reshape(256, CHIP).T
        ht[...] = hid[k, :, :, 0:FF].reshape(256, FF).T

        @pl.loop(0, 7)
        def _(n):
            cols = pl.ds(pl.multiple_of(n * 256, 256), 256)
            from_cols = pl.ds(pl.multiple_of(FF + n * 256, 128), 256)
            pulled = hid[k, :, :, from_cols].reshape(256, 256)
            for m in range(4):
                acc_gu[m * 256 : m * 256 + 256, cols] += mm(xt[m * 256 : m * 256 + 256, :], pulled)

        @pl.loop(0, 4)
        def _(n):
            cols = pl.ds(pl.multiple_of(n * 256, 256), 256)
            from_cols = pl.ds(pl.multiple_of(CHIP + n * 256, 256), 256)
            cots = gath[k, :, :, :, from_cols].reshape(256, 256)
            for m, high in ((0, 256), (256, 256), (512, 256), (768, 128)):
                acc_d[m : m + high, cols] += mm(ht[m : m + high, :], cots)

    def sum_first(k, a):
        s = k % 2
        for i in range(4):
            for h in range(2):
                total = (outp[s, i, x, :, strip(a, 0)] if h == 0 else outp[s, z, i, :, strip(a, 1)]).astype(F32)
                for j in range(3):
                    total += rs1[k, a, h, j, i].astype(F32)
                sum1[k, a, h, i] = total.astype(BF)

    def sum_last(k, a):
        to = bw if a == 1 else fw
        rows = pl.ds(pl.multiple_of(k * TOK, TOK), TOK)
        for h in range(2):
            total = sum1[k, a, h, z if h == 0 else x].astype(F32)
            for j in range(3):
                total += rs2[k, a, h, j].astype(F32)
            to[rows, h * WIDE : (h + 1) * WIDE] = total

    exchange = [
        rc(send_gu, recv_gu, w_s.at[0], w_r.at[0], twin),
        rc(send_d, recv_d, w_s.at[1], w_r.at[1], twin),
    ]

    def step(i, carry):
        def at(k):
            return jnp.logical_and(k >= 0, k < CHUNKS)

        @pl.when(at(i - 2))
        def _():
            k = i - 2
            finish(quarter(k, k % 2, 1))
            finish(quarter(k, k % 2, 0))
            activate(k)
            start(share(k, 0))
            start(share(k, 1))

        @pl.when(at(i - 1))
        def _():
            k = i - 1
            for a in (1, 0):
                finish(relay(k, k % 2, a))
                add_relay(k, a)
                start(quarter(k, k % 2, a))

        @pl.when(i < CHUNKS)
        def _():
            finish(rest(i, 1))
            project_back(i)
            start(relay(i, i % 2, 1))
            finish(rest(i, 0))
            project_pre(i)
            start(relay(i, i % 2, 0))

        @pl.when(i + 1 < CHUNKS)
        def _():
            for a in (1, 0):
                finish(near(i + 1, a))
                start(rest(i + 1, a))

        @pl.when(i + 2 < CHUNKS)
        def _():
            start(near(i + 2, 1) + near(i + 2, 0))

        @pl.when(at(i - 4))
        def _():
            k = i - 4
            for a in (1, 0):
                finish(scatter(k, k % 2, a))
                sum_first(k, a)
                start(scatter_rest(k, a))

        @pl.when(at(i - 3))
        def _():
            k = i - 3
            finish(share(k, 1) + pass_on(k))
            products_back(k)
            start(scatter(k, k % 2, 1))
            products_out(k)
            start(scatter(k, k % 2, 0))
            weight_sums(k)

        @pl.when(i - 3 == CHUNKS - 1)
        def _():
            @pl.loop(0, 4)
            def _(n):
                rows = pl.ds(pl.multiple_of(n * 128, 128), 128)
                src = pl.ds(pl.multiple_of(other * WIDE + n * 128, 128), 128)
                send_gu[rows, :] = acc_gu[src, :].astype(BF)

            send_d[...] = acc_d[:, theirs].astype(BF)
            start(exchange)

        @pl.when(at(i - 5))
        def _():
            for a in (1, 0):
                finish(scatter_rest(i - 5, a))
                sum_last(i - 5, a)

        @pl.when(at(i - 2))
        def _():
            finish(share(i - 2, 0))
            start(pass_on(i - 2))

        return carry

    lax.fori_loop(0, CHUNKS + 4, step, 0)

    finish(scatter_rest(CHUNKS - 1, 1))
    sum_last(CHUNKS - 1, 1)
    inv = invb[:, 0:1]
    pull = jnp.sum(tokb[...].astype(F32) * gainb[0:1, :] * bw[...], axis=1, keepdims=True)
    rmsb[y] = to_lanes(pull * inv)
    sends = [rc(rmsb.at[y], rmsb.at[y], m_s.at[j - 1], m_r.at[j - 1], ydev(j)) for j in (1, 2, 3)]
    start(sends)
    finish(scatter_rest(CHUNKS - 1, 0))
    sum_last(CHUNKS - 1, 0)
    mixb[...] = (tokb[...].astype(F32) + fw[...]).astype(BF)
    back = [
        rc(mixb.at[:, theirs], mixed_ref.at[my_rows, :], o_s.at[0], o_r.at[0], twin),
        rc(igb.at[:, theirs], ig_ref.at[my_rows, :], o_s.at[1], o_r.at[1], twin),
    ]
    start(back[0:1])
    mixed_ref[my_rows, :] = mixb[:, mine]
    finish(sends)
    fix = inv * inv * to_column(((rmsb[0] + rmsb[1]) + (rmsb[2] + rmsb[3]))[0:1, :]) / MODEL
    igb[...] = (
        cotb[...].astype(F32) + gainb[0:1, :] * (inv * bw[...]) - tokb[...].astype(F32) * fix
    ).astype(BF)
    start(back[1:2])
    ig_ref[my_rows, :] = igb[:, mine]

    finish(exchange)

    @pl.loop(0, 4)
    def _(i):
        rows = pl.ds(pl.multiple_of(i * 128, 128), 128)
        src = pl.ds(pl.multiple_of(c * WIDE + i * 128, 128), 128)
        for j in range(7):
            cols = slice(j * 128, j * 128 + 128)
            wide = slice(FF + j * 128, FF + j * 128 + 128)
            total = acc_gu[src, cols] + recv_gu[rows, cols].astype(F32)
            gg_ref[rows, cols] = (total * gm_ref[i, j].astype(F32)).astype(BF)
            total = acc_gu[src, wide] + recv_gu[rows, wide].astype(F32)
            ug_ref[rows, cols] = (total * um_ref[i, j].astype(F32)).astype(BF)

    @pl.loop(0, 7)
    def _(i):
        rows = pl.ds(pl.multiple_of(i * 128, 128), 128)
        for j in range(4):
            cols = slice(j * 128, j * 128 + 128)
            src = pl.ds(pl.multiple_of(c * WIDE + j * 128, 128), 128)
            total = acc_d[rows, src] + recv_d[rows, cols].astype(F32)
            dg_ref[rows, cols] = (total * dm_ref[j, i].astype(F32)).astype(BF)

    finish(back)


def store(*refs):
    copies = [pltpu.make_async_copy(refs[i], refs[5 + i], refs[10].at[i]) for i in range(5)]
    for copy in copies:
        copy.start()
    for copy in copies:
        copy.wait()


def shards(tokens, cotangent, norm_gain, gate_w, up_w, down_w, gate_b, up_b, down_b):
    vmem = pl.BlockSpec(memory_space=pltpu.VMEM)
    smem = pl.BlockSpec(memory_space=pltpu.SMEM)

    def dma(*shape):
        return [pltpu.SemaphoreType.DMA(shape)] * 2

    V = pltpu.VMEM
    results = pl.pallas_call(
        body,
        out_shape=(
            V(tokens.shape, BF),
            V(tokens.shape, BF),
            V(gate_w.shape, BF),
            V(up_w.shape, BF),
            V(down_w.shape, BF),
        ),
        in_specs=[vmem] * 6 + [smem] * 3,
        out_specs=(vmem,) * 5,
        scratch_shapes=[
            V((HALF, CHIP), BF),
            V((HALF, CHIP), BF),
            V((8, WIDE), F32),
            V((8, CHIP), F32),
            V((4, 8, 128), F32),
            V((HALF, 128), F32),
            V((4, 8, 128), F32),
            V((CHUNKS, 4, 4, TOK, 2 * CHIP), BF),
            V((CHIP, GU), BF),
            V((FF, CHIP), BF),
            V((2, 4, 64, ALL), BF),
            V((CHUNKS, 2, 32, ALL), BF),
            V((CHUNKS, 2, 64, ALL), BF),
            V((CHUNKS, 4, 64, ALL), BF),
            V((2, 4, 4, TOK, 2 * CHIP), BF),
            V((CHUNKS, 2, 2, 3, 4, TOK, WIDE), BF),
            V((CHUNKS, 2, 2, 4, TOK, WIDE), BF),
            V((CHUNKS, 2, 2, 3, TOK, WIDE), BF),
            V((HALF, CHIP), F32),
            V((HALF, CHIP), F32),
            V((CHIP, GU), F32),
            V((FF, CHIP), F32),
            V((CHIP, 256), BF),
            V((FF, 256), BF),
            V((WIDE, GU), BF),
            V((FF, WIDE), BF),
            V((WIDE, GU), BF),
            V((FF, WIDE), BF),
            V((HALF, CHIP), BF),
            V((HALF, CHIP), BF),
        ]
        + dma(5)
        + dma(3)
        + dma(CHUNKS, 2, 2, 3)
        + dma(CHUNKS, 2, 2, 3)
        + dma(CHUNKS, 2, 2)
        + dma(CHUNKS, 2, 2)
        + dma(CHUNKS, 2, 2)
        + dma(CHUNKS, 2)
        + dma(CHUNKS, 2, 2, 3)
        + dma(CHUNKS, 2, 2, 3)
        + dma(2)
        + dma(3)
        + dma(2),
        compiler_params=pltpu.CompilerParams(
            collective_id=0, has_side_effects=True, vmem_limit_bytes=54 * 1024 * 1024
        ),
        cost_estimate=pl.CostEstimate(flops=17_000_000_000, bytes_accessed=6_000_000, transcendentals=2_000_000),
        name="ffn",
    )(tokens, cotangent, norm_gain.reshape(1, -1), gate_w, up_w, down_w, gate_b, up_b, down_b.T)
    return pl.pallas_call(
        store,
        out_shape=tuple(jax.ShapeDtypeStruct(r.shape, r.dtype) for r in results),
        in_specs=[vmem] * 5,
        out_specs=(pl.BlockSpec(memory_space=pl.ANY),) * 5,
        scratch_shapes=[pltpu.SemaphoreType.DMA((5,))],
        name="store",
    )(*[pltpu.with_memory_space_constraint(r, pltpu.VMEM) for r in results])


def solution(mesh):
    in_specs = (
        P("row", "col"),
        P("row", "col"),
        P("col"),
        P("col", "row"),
        P("col", "row"),
        P("row", "col"),
        P("col", "row"),
        P("col", "row"),
        P("row", "col"),
    )
    out_specs = (
        P("row", "col"),
        P("row", "col"),
        P("col", "row"),
        P("col", "row"),
        P("row", "col"),
    )
    return jax.shard_map(shards, mesh=mesh, in_specs=in_specs, out_specs=out_specs, check_vma=False)
```

```python
import jax
import jax.numpy as jnp
from jax import lax
from jax.experimental import pallas as pl
from jax.experimental.pallas import tpu as pltpu
from jax.sharding import PartitionSpec as P

epsilon = 1e-05
MESH = pl.DeviceIdType.MESH
BF = jnp.bfloat16
F32 = jnp.float32

CHUNKS = 4
TOK = 16
HALF = 64
WIDE = 512
CHIP = 1024
FF = 896
GU = 2 * FF
ALL = 3 * FF
MODEL = 4096


def mm(a, b):
    return jnp.dot(a, b, preferred_element_type=F32)


def mm_nt(a, b):
    return lax.dot_general(a, b, (((1,), (1,)), ((), ())), preferred_element_type=F32)


def body(
    tok_ref, cot_ref, gain_ref, gw_ref, uw_ref, dw_ref, gm_ref, um_ref, dm_ref,
    mixed_ref, ig_ref, gg_ref, ug_ref, dg_ref,
    gwb, uwb, dwb, tokn, cotn, tokb, cotb, gain8, gainb, ssq, invb, invn, pulls, totals,
    gath, wgu, wd, part, rel, full, hid, outp, rs1, sum1, rs2,
    acc_gu, acc_d, xt, ht, send_gu, send_d, recv_gu, recv_d,
    l_s, sw_s, sw_r, sq_s, sq_r, p1_s, p1_r, p2_s, p2_r, r_s, r_r, f_s, f_r, t_s, t_r, g_s, g_r, h_s, h_r,
    a_s, a_r, b_s, b_r, w_s, w_r,
):
    row = lax.axis_index("row")
    col = lax.axis_index("col")
    z, x, y, c = row // 4, row % 4, col // 2, col % 2
    other = 1 - c
    up, dn, op = (y + 1) % 4, (y + 3) % 4, (y + 2) % 4

    def dev(dz, dx, dy, dc):
        return (dz * 4 + dx, dy * 2 + dc)

    twin = dev(z, x, y, other)
    up_dev, dn_dev = dev(z, x, up, c), dev(z, x, dn, c)

    def zdev(j):
        return dev((z + j) % 4, x, y, c)

    def xdev(j):
        return dev(z, (x + j) % 4, y, c)

    def ydev(j):
        return dev(z, x, (y + j) % 4, c)

    def rc(src, dst, ss, rs, to):
        return pltpu.make_async_remote_copy(
            src_ref=src, dst_ref=dst, send_sem=ss, recv_sem=rs, device_id=to, device_id_type=MESH
        )

    def start(copies):
        for copy in copies:
            copy.start()

    def finish(copies):
        for copy in copies:
            copy.wait()

    lo = pl.ds(0, CHIP)
    hi = pl.ds(CHIP, CHIP)

    def strip(a, h):
        return pl.ds(a * CHIP + h * WIDE, WIDE)

    spot = lax.broadcasted_iota(jnp.int32, (HALF, 128), 0) == lax.broadcasted_iota(jnp.int32, (HALF, 128), 1)

    def to_lanes(column):
        line = jnp.sum(jnp.where(spot, jnp.broadcast_to(column, (HALF, 128)), 0.0), axis=0, keepdims=True)
        return jnp.broadcast_to(line, (8, 128))

    def to_column(line):
        return jnp.sum(jnp.where(spot, jnp.broadcast_to(line, (HALF, 128)), 0.0), axis=1, keepdims=True)

    mine = pl.ds(pl.multiple_of(c * WIDE, WIDE), WIDE)
    theirs = pl.ds(pl.multiple_of(other * WIDE, WIDE), WIDE)
    my_rows = pl.ds(pl.multiple_of(c * HALF, HALF), HALF)
    their_rows = pl.ds(pl.multiple_of(other * HALF, HALF), HALF)

    def width(a):
        return WIDE + 128 * (1 - a)

    def out_strip(a, h):
        return pl.ds(2 * (WIDE + 128) * a + h * width(a), width(a))

    barrier = pltpu.get_barrier_semaphore()
    peers = [twin] + [f(j) for f in (xdev, ydev, zdev) for j in (1, 2, 3)]
    peers += [dev((z + j) % 4, x, y, other) for j in (1, 2, 3)] + [dev(z, (x + j) % 4, y, other) for j in (1, 2, 3)]
    for peer in peers:
        pl.semaphore_signal(barrier, inc=1, device_id=peer, device_id_type=MESH)

    loads = [
        pltpu.make_async_copy(src, dst, l_s.at[n])
        for n, (src, dst) in enumerate(
            ((cot_ref, cotn), (tok_ref, tokn), (dw_ref, dwb), (gw_ref, gwb), (uw_ref, uwb))
        )
    ]
    start(loads)
    gain8[...] = jnp.broadcast_to(gain_ref[...], (8, WIDE))
    gainb[:, mine] = gain8[...]
    finish(loads[0:2])
    tokb[:, mine] = tokn[my_rows, :]
    cotb[:, mine] = cotn[my_rows, :]
    finish(loads[2:3])

    @pl.loop(0, 7)
    def _(i):
        rows = pl.ds(pl.multiple_of(i * 128, 128), 128)
        for j in range(4):
            to = pl.ds(pl.multiple_of(c * WIDE + j * 128, 128), 128)
            keep = dm_ref[j, i].astype(F32)
            wd[rows, to] = (dwb[rows, j * 128 : j * 128 + 128].astype(F32) * keep).astype(BF)

    pl.semaphore_wait(barrier, len(peers))

    swaps = [
        rc(cotn.at[their_rows, :], cotb.at[:, mine], sw_s.at[0], sw_r.at[0], twin),
        rc(tokn.at[their_rows, :], tokb.at[:, mine], sw_s.at[1], sw_r.at[1], twin),
        rc(gain8, gainb.at[:, mine], sw_s.at[2], sw_r.at[2], twin),
        rc(wd.at[:, mine], wd.at[:, mine], sw_s.at[3], sw_r.at[3], twin),
        rc(wgu.at[mine, :], wgu.at[mine, :], sw_s.at[4], sw_r.at[4], twin),
        rc(invn.at[my_rows, :], invn.at[my_rows, :], sw_s.at[5], sw_r.at[5], twin),
    ]
    start(swaps[0:4])

    def near(k, a):
        def one(h, to, j):
            block = gath.at[k, z, x, :, strip(a, h)]
            return rc(block, block, p1_s.at[k, a, h, j - 1], p1_r.at[k, a, h, j - 1], to(j))

        return [one(h, to, j) for j in (1, 2, 3) for h, to in ((0, xdev), (1, zdev))]

    def rest(k, a):
        def one(h, to, j):
            block = gath.at[k, z, :, :, strip(a, 0)] if h == 0 else gath.at[k, :, x, :, strip(a, 1)]
            return rc(block, block, p2_s.at[k, a, h, j - 1], p2_r.at[k, a, h, j - 1], to(j))

        return [one(h, to, j) for j in (1, 2, 3) for h, to in ((0, zdev), (1, xdev))]

    finish(swaps[0:1])
    for k in range(CHUNKS):
        gath[k, z, x, :, hi] = cotb[k * TOK : (k + 1) * TOK, :]
    start(near(0, 1))

    finish(swaps[1:3])
    tok = tokb[...].astype(F32)
    ssq[y] = to_lanes(jnp.sum(tok * tok, axis=1, keepdims=True))
    sends = [rc(ssq.at[y], ssq.at[y], sq_s.at[j - 1], sq_r.at[j - 1], ydev(j)) for j in (1, 2, 3)]
    start(sends)
    finish(loads[3:5])

    @pl.loop(0, 4)
    def _(i):
        rows = pl.ds(pl.multiple_of(i * 128, 128), 128)
        to = pl.ds(pl.multiple_of(c * WIDE + i * 128, 128), 128)
        for j in range(7):
            cols = slice(j * 128, j * 128 + 128)
            keep = gm_ref[i, j].astype(F32)
            wgu[to, j * 128 : j * 128 + 128] = (gwb[rows, cols].astype(F32) * keep).astype(BF)
            keep = um_ref[i, j].astype(F32)
            wgu[to, FF + j * 128 : FF + j * 128 + 128] = (uwb[rows, cols].astype(F32) * keep).astype(BF)

    start(swaps[4:5])
    finish(near(0, 1))
    start(rest(0, 1))
    finish(sends)
    squares = to_column(((ssq[0] + ssq[1]) + (ssq[2] + ssq[3]))[0:1, :])
    invb[...] = jnp.broadcast_to(1.0 / jnp.sqrt(squares / MODEL + epsilon), (HALF, 128))
    for k in range(CHUNKS):
        rows = slice(k * TOK, (k + 1) * TOK)
        scaled = tokb[rows, :].astype(F32) * gainb[0:1, :] * invb[rows, 0:1]
        gath[k, z, x, :, lo] = scaled.astype(BF)
    start(near(0, 0))
    invn[my_rows, :] = invb[...]
    start(swaps[5:6])

    @pl.loop(0, 16)
    def _(i):
        acc_gu[pl.ds(pl.multiple_of(i * 64, 64), 64), :] = jnp.zeros((64, GU), F32)
        acc_d[pl.ds(pl.multiple_of(i * 56, 56), 56), :] = jnp.zeros((56, CHIP), F32)

    finish(near(0, 0))
    start(rest(0, 0))
    start(near(1, 1) + near(1, 0))
    finish(swaps[3:6])

    def span(a):
        return pl.ds(GU, FF) if a == 1 else pl.ds(0, GU)

    def relay(k, s, a):
        one = part.at[s, op, pl.ds(0, 32), span(a)]
        two = part.at[s, op, pl.ds(32, 32), span(a)]
        return [
            rc(one, rel.at[k, 0, :, span(a)], r_s.at[k, a, 0], r_r.at[k, a, 0], up_dev),
            rc(two, rel.at[k, 1, :, span(a)], r_s.at[k, a, 1], r_r.at[k, a, 1], dn_dev),
        ]

    def quarter(k, s, a):
        return [
            rc(part.at[s, up, :, span(a)], full.at[k, 0, :, span(a)], f_s.at[k, a, 0], f_r.at[k, a, 0], up_dev),
            rc(part.at[s, dn, :, span(a)], full.at[k, 1, :, span(a)], f_s.at[k, a, 1], f_r.at[k, a, 1], dn_dev),
        ]

    def kind(b):
        return pl.ds(FF, GU) if b == 1 else pl.ds(0, FF)

    def share(k, b, later):
        one = hid.at[k, y, pl.ds(32 if later else 0, 32), kind(b)]
        two = hid.at[k, y, pl.ds(0 if later else 32, 32), kind(b)]
        return [
            rc(one, one, g_s.at[k, b, later, 0], g_r.at[k, b, later, 0], up_dev),
            rc(two, two, g_s.at[k, b, later, 1], g_r.at[k, b, later, 1], dn_dev),
        ]

    def pass_on(k, b):
        first = hid.at[k, dn, pl.ds(0, 32), kind(b)]
        second = hid.at[k, up, pl.ds(32, 32), kind(b)]
        return [
            rc(first, first, h_s.at[k, b, 0], h_r.at[k, b, 0], up_dev),
            rc(second, second, h_s.at[k, b, 1], h_r.at[k, b, 1], dn_dev),
        ]

    def tell(k):
        return [rc(pulls.at[k, y], pulls.at[k, y], t_s.at[k, j - 1], t_r.at[k, j - 1], ydev(j)) for j in (1, 2, 3)]

    def scatter(k, s, a):
        def one(h, to, j):
            strip_a = out_strip(a, h)
            block = outp.at[s, :, (x + j) % 4, :, strip_a] if h == 0 else outp.at[s, (z + j) % 4, :, :, strip_a]
            return rc(
                block, rs1.at[k, a, h, j - 1, :, :, pl.ds(0, width(a))],
                a_s.at[k, a, h, j - 1], a_r.at[k, a, h, j - 1], to(j),
            )

        return [one(h, to, j) for j in (1, 2, 3) for h, to in ((0, xdev), (1, zdev))]

    at_mine = z * other + x * c
    at_theirs = z * c + x * other

    def scatter_rest(k, a):
        def one(h, place, send, j, to):
            return rc(
                sum1.at[k, a, h, place, :, pl.ds(0, width(a))], rs2.at[k, a, c, j, :, pl.ds(0, width(a))],
                send, b_r.at[k, a, c, j], to,
            )

        far = [
            one(h, ((x if h else z) + j) % 4, b_s.at[k, a, h, j], j,
                dev(z, (x + j) % 4, y, 1) if h else dev((z + j) % 4, x, y, 0))
            for j in (1, 2, 3) for h in (0, 1)
        ]
        return far + [one(other, at_theirs, b_s.at[k, a, 0, 0], 0, twin)]

    def await_rest(k, a):
        for copy in scatter_rest(k, a):
            copy.wait_send()

        def arrival(core, j):
            place = rs2.at[k, a, core, j, :, pl.ds(0, width(a))]
            rc(place, place, b_s.at[k, a, 0, 0], b_r.at[k, a, core, j], twin).wait_recv()

        arrival(other, 0)
        for j in (1, 2, 3):
            arrival(0, j)
            arrival(1, j)

    def project_pre(k):
        s = k % 2

        @pl.loop(0, 7)
        def _(n):
            cols = pl.ds(pl.multiple_of(n * 256, 256), 256)
            got = mm(gath[k, :, :, :, lo].reshape(256, CHIP), wgu[:, cols])
            part[s, :, :, cols] = got.astype(BF).reshape(4, 64, 256)

    def project_back(k):
        s = k % 2
        for n, wide in ((0, 256), (256, 256), (512, 256), (768, 128)):
            got = mm_nt(gath[k, :, :, :, hi].reshape(256, CHIP), wd[n : n + wide, :])
            part[s, :, :, GU + n : GU + n + wide] = got.astype(BF).reshape(4, 64, wide)

    def add_relay(k, a):
        s = k % 2
        base, count = (GU, 7) if a == 1 else (0, 14)

        @pl.loop(0, count)
        def _(n):
            cols = pl.ds(pl.multiple_of(base + n * 128, 128), 128)
            part[s, up, 0:32, cols] = (part[s, up, 0:32, cols].astype(F32) + rel[k, 0, :, cols].astype(F32)).astype(BF)
            part[s, dn, 32:64, cols] = (part[s, dn, 32:64, cols].astype(F32) + rel[k, 1, :, cols].astype(F32)).astype(BF)

    def activate(k):
        s = k % 2

        def one(n, pulled):
            def total(base):
                cols = pl.ds(pl.multiple_of(base + n * 128, 128), 128)
                return part[s, y, :, cols].astype(F32) + full[k, 0, :, cols].astype(F32) + full[k, 1, :, cols].astype(F32)

            gate, up_value, back = total(0), total(FF), total(GU)
            sigma = jax.nn.sigmoid(gate)
            activ = gate * sigma
            d_gate = back * up_value * sigma * (1.0 + gate * (1.0 - sigma))
            d_up = back * activ
            hid[k, y, :, pl.ds(pl.multiple_of(n * 128, 128), 128)] = (activ * up_value).astype(BF)
            hid[k, y, :, pl.ds(pl.multiple_of(FF + n * 128, 128), 128)] = d_gate.astype(BF)
            hid[k, y, :, pl.ds(pl.multiple_of(GU + n * 128, 128), 128)] = d_up.astype(BF)
            return pulled + (d_gate * gate + d_up * up_value)

        pulled = lax.fori_loop(0, 7, one, jnp.zeros((HALF, 128), F32))
        pulls[k, y] = to_lanes(jnp.sum(pulled, axis=1, keepdims=True))

    def products_back(k):
        s = k % 2

        @pl.loop(0, 4)
        def _(n):
            cols = pl.ds(pl.multiple_of(n * 256, 256), 256)
            got = mm_nt(hid[k, :, :, FF:ALL].reshape(256, GU), wgu[cols, :])
            outp[s, :, :, :, pl.ds(pl.multiple_of(2 * (WIDE + 128) + n * 256, 256), 256)] = got.astype(BF).reshape(4, 4, TOK, 256)

    def products_out(k):
        s = k % 2

        @pl.loop(0, 4)
        def _(n):
            cols = pl.ds(pl.multiple_of(n * 256, 256), 256)
            got = mm(hid[k, :, :, 0:FF].reshape(256, FF), wd[:, cols])
            to = pl.ds(pl.multiple_of(n * 256 + (n // 2) * 128, 128), 256)
            outp[s, :, :, :, to] = got.astype(BF).reshape(4, 4, TOK, 256)

        for i in range(4):
            pulled = jnp.broadcast_to(to_column(pulls[k, i, 0:1, :]), (HALF, 128)).astype(BF).reshape(4, TOK, 128)
            outp[s, i, :, :, WIDE : WIDE + 128] = pulled
            outp[s, i, :, :, 2 * WIDE + 128 : 2 * WIDE + 256] = pulled

    def sums_gu(k):
        xt[...] = gath[k, :, :, :, lo].reshape(256, CHIP).T

        @pl.loop(0, 7)
        def _(n):
            cols = pl.ds(pl.multiple_of(n * 256, 256), 256)
            from_cols = pl.ds(pl.multiple_of(FF + n * 256, 128), 256)
            pulled = hid[k, :, :, from_cols].reshape(256, 256)
            for m in range(4):
                acc_gu[m * 256 : m * 256 + 256, cols] += mm(xt[m * 256 : m * 256 + 256, :], pulled)

    def sums_d(k):
        ht[...] = hid[k, :, :, 0:FF].reshape(256, FF).T

        @pl.loop(0, 4)
        def _(n):
            cols = pl.ds(pl.multiple_of(n * 256, 256), 256)
            from_cols = pl.ds(pl.multiple_of(CHIP + n * 256, 256), 256)
            cots = gath[k, :, :, :, from_cols].reshape(256, 256)
            for m, high in ((0, 256), (256, 256), (512, 256), (768, 128)):
                acc_d[m : m + high, cols] += mm(ht[m : m + high, :], cots)

    def sum_first(k, a):
        s = k % 2
        for i in range(4):
            for h in range(2):
                total = (outp[s, i, x, :, out_strip(a, 0)] if h == 0 else outp[s, z, i, :, out_strip(a, 1)]).astype(F32)
                for j in range(3):
                    total += rs1[k, a, h, j, i, :, 0 : width(a)].astype(F32)
                sum1[k, a, h, i, :, 0 : width(a)] = total.astype(BF)

    def sum_last(k, a):
        for core, first in ((c, sum1[k, a, c, at_mine, :, 0 : width(a)]), (other, rs2[k, a, other, 0, :, 0 : width(a)])):
            rows = pl.ds(pl.multiple_of(core * HALF + k * TOK, TOK), TOK)
            total = first.astype(F32)
            for j in (1, 2, 3):
                total += rs2[k, a, core, j, :, 0 : width(a)].astype(F32)
            if a == 0:
                mixed_ref[rows, :] = (tokn[rows, :].astype(F32) + total[:, 0:WIDE]).astype(BF)
                totals[rows, :] = total[:, WIDE:]
            else:
                inv = invn[rows, 0:1]
                fix = inv * inv * totals[rows, 0:1] / MODEL
                ig_ref[rows, :] = (
                    cotn[rows, :].astype(F32) + gain8[0:1, :] * (inv * total) - tokn[rows, :].astype(F32) * fix
                ).astype(BF)

    exchange = [
        rc(send_gu, recv_gu, w_s.at[0], w_r.at[0], twin),
        rc(send_d, recv_d, w_s.at[1], w_r.at[1], twin),
    ]

    def step(i, carry):
        def at(k):
            return jnp.logical_and(k >= 0, k < CHUNKS)

        @pl.when(at(i - 2))
        def _():
            k = i - 2
            finish(quarter(k, k % 2, 1))
            finish(quarter(k, k % 2, 0))
            activate(k)
            start(tell(k))
            for b in (0, 1):
                start(share(k, b, 0) + share(k, b, 1))

        @pl.when(at(i - 1))
        def _():
            k = i - 1
            for a in (1, 0):
                finish(relay(k, k % 2, a))
                add_relay(k, a)
                start(quarter(k, k % 2, a))

        @pl.when(i < CHUNKS)
        def _():
            finish(rest(i, 1))
            project_back(i)
            start(relay(i, i % 2, 1))
            finish(rest(i, 0))
            project_pre(i)
            start(relay(i, i % 2, 0))

        @pl.when(i + 1 < CHUNKS)
        def _():
            for a in (1, 0):
                finish(near(i + 1, a))
                start(rest(i + 1, a))

        @pl.when(i + 2 < CHUNKS)
        def _():
            start(near(i + 2, 1) + near(i + 2, 0))

        @pl.when(at(i - 4))
        def _():
            k = i - 4
            for a in (0, 1):
                finish(scatter(k, k % 2, a))
                sum_first(k, a)
                start(scatter_rest(k, a))

        @pl.when(at(i - 3))
        def _():
            k = i - 3
            finish(tell(k) + share(k, 0, 1) + pass_on(k, 0))
            products_out(k)
            start(scatter(k, k % 2, 0))
            sums_d(k)

        @pl.when(i - 3 == CHUNKS - 1)
        def _():
            send_d[...] = acc_d[:, theirs].astype(BF)
            start(exchange[1:])

        @pl.when(at(i - 3))
        def _():
            k = i - 3
            finish(share(k, 1, 1) + pass_on(k, 1))
            products_back(k)
            start(scatter(k, k % 2, 1))
            sums_gu(k)

        @pl.when(i - 3 == CHUNKS - 1)
        def _():
            @pl.loop(0, 4)
            def _(n):
                rows = pl.ds(pl.multiple_of(n * 128, 128), 128)
                src = pl.ds(pl.multiple_of(other * WIDE + n * 128, 128), 128)
                send_gu[rows, :] = acc_gu[src, :].astype(BF)

            start(exchange[0:1])

        @pl.when(at(i - 5))
        def _():
            for a in (0, 1):
                await_rest(i - 5, a)
                sum_last(i - 5, a)

        @pl.when(at(i - 2))
        def _():
            for b in (0, 1):
                finish(share(i - 2, b, 0))
                start(pass_on(i - 2, b))

        return carry

    lax.fori_loop(0, CHUNKS + 4, step, 0)

    await_rest(CHUNKS - 1, 0)
    sum_last(CHUNKS - 1, 0)
    finish(exchange)

    @pl.loop(0, 4)
    def _(i):
        rows = pl.ds(pl.multiple_of(i * 128, 128), 128)
        src = pl.ds(pl.multiple_of(c * WIDE + i * 128, 128), 128)
        for j in range(7):
            cols = slice(j * 128, j * 128 + 128)
            wide = slice(FF + j * 128, FF + j * 128 + 128)
            total = acc_gu[src, cols] + recv_gu[rows, cols].astype(F32)
            gg_ref[rows, cols] = (total * gm_ref[i, j].astype(F32)).astype(BF)
            total = acc_gu[src, wide] + recv_gu[rows, wide].astype(F32)
            ug_ref[rows, cols] = (total * um_ref[i, j].astype(F32)).astype(BF)

    @pl.loop(0, 7)
    def _(i):
        rows = pl.ds(pl.multiple_of(i * 128, 128), 128)
        for j in range(4):
            cols = slice(j * 128, j * 128 + 128)
            src = pl.ds(pl.multiple_of(c * WIDE + j * 128, 128), 128)
            total = acc_d[rows, src] + recv_d[rows, cols].astype(F32)
            dg_ref[rows, cols] = (total * dm_ref[j, i].astype(F32)).astype(BF)

    await_rest(CHUNKS - 1, 1)
    sum_last(CHUNKS - 1, 1)


def store(*refs):
    copies = [pltpu.make_async_copy(refs[i], refs[5 + i], refs[10].at[i]) for i in range(5)]
    for copy in copies:
        copy.start()
    for copy in copies:
        copy.wait()


def shards(tokens, cotangent, norm_gain, gate_w, up_w, down_w, gate_b, up_b, down_b):
    vmem = pl.BlockSpec(memory_space=pltpu.VMEM)
    smem = pl.BlockSpec(memory_space=pltpu.SMEM)
    hbm = pl.BlockSpec(memory_space=pltpu.HBM)

    def dma(*shape):
        return [pltpu.SemaphoreType.DMA(shape)] * 2

    V = pltpu.VMEM
    results = pl.pallas_call(
        body,
        out_shape=(
            V(tokens.shape, BF),
            V(tokens.shape, BF),
            V(gate_w.shape, BF),
            V(up_w.shape, BF),
            V(down_w.shape, BF),
        ),
        in_specs=[hbm, hbm, vmem, hbm, hbm, hbm] + [smem] * 3,
        out_specs=(vmem,) * 5,
        scratch_shapes=[
            V((WIDE, FF), BF),
            V((WIDE, FF), BF),
            V((FF, WIDE), BF),
            V((2 * HALF, WIDE), BF),
            V((2 * HALF, WIDE), BF),
            V((HALF, CHIP), BF),
            V((HALF, CHIP), BF),
            V((8, WIDE), F32),
            V((8, CHIP), F32),
            V((4, 8, 128), F32),
            V((HALF, 128), F32),
            V((2 * HALF, 128), F32),
            V((CHUNKS, 4, 8, 128), F32),
            V((2 * HALF, 128), F32),
            V((CHUNKS, 4, 4, TOK, 2 * CHIP), BF),
            V((CHIP, GU), BF),
            V((FF, CHIP), BF),
            V((2, 4, 64, ALL), BF),
            V((CHUNKS, 2, 32, ALL), BF),
            V((CHUNKS, 2, 64, ALL), BF),
            V((CHUNKS, 4, 64, ALL), BF),
            V((2, 4, 4, TOK, 2 * (WIDE + 128) + CHIP), BF),
            V((CHUNKS, 2, 2, 3, 4, TOK, WIDE + 128), BF),
            V((CHUNKS, 2, 2, 4, TOK, WIDE + 128), BF),
            V((CHUNKS, 2, 2, 4, TOK, WIDE + 128), BF),
            V((CHIP, GU), F32),
            V((FF, CHIP), F32),
            V((CHIP, 256), BF),
            V((FF, 256), BF),
            V((WIDE, GU), BF),
            V((FF, WIDE), BF),
            V((WIDE, GU), BF),
            V((FF, WIDE), BF),
            pltpu.SemaphoreType.DMA((5,)),
        ]
        + dma(6)
        + dma(3)
        + dma(CHUNKS, 2, 2, 3)
        + dma(CHUNKS, 2, 2, 3)
        + dma(CHUNKS, 2, 2)
        + dma(CHUNKS, 2, 2)
        + dma(CHUNKS, 3)
        + dma(CHUNKS, 2, 2, 2)
        + dma(CHUNKS, 2, 2)
        + dma(CHUNKS, 2, 2, 3)
        + dma(CHUNKS, 2, 2, 4)
        + dma(2),
        compiler_params=pltpu.CompilerParams(
            collective_id=0, has_side_effects=True, vmem_limit_bytes=56 * 1024 * 1024
        ),
        cost_estimate=pl.CostEstimate(flops=17_000_000_000, bytes_accessed=6_000_000, transcendentals=2_000_000),
        name="ffn",
    )(tokens, cotangent, norm_gain.reshape(1, -1), gate_w, up_w, down_w, gate_b, up_b, down_b.T)
    return pl.pallas_call(
        store,
        out_shape=tuple(jax.ShapeDtypeStruct(r.shape, r.dtype) for r in results),
        in_specs=[vmem] * 5,
        out_specs=(pl.BlockSpec(memory_space=pl.ANY),) * 5,
        scratch_shapes=[pltpu.SemaphoreType.DMA((5,))],
        name="store",
    )(*[pltpu.with_memory_space_constraint(r, pltpu.VMEM) for r in results])


def solution(mesh):
    in_specs = (
        P("row", "col"),
        P("row", "col"),
        P("col"),
        P("col", "row"),
        P("col", "row"),
        P("row", "col"),
        P("col", "row"),
        P("col", "row"),
        P("row", "col"),
    )
    out_specs = (
        P("row", "col"),
        P("row", "col"),
        P("col", "row"),
        P("col", "row"),
        P("row", "col"),
    )
    return jax.shard_map(shards, mesh=mesh, in_specs=in_specs, out_specs=out_specs, check_vma=False)
```

```python
import jax
import jax.numpy as jnp
from jax import lax
from jax.experimental import pallas as pl
from jax.experimental.pallas import tpu as pltpu
from jax.sharding import PartitionSpec as P

epsilon = 1e-05
MESH = pl.DeviceIdType.MESH
BF = jnp.bfloat16
F32 = jnp.float32

CHUNKS = 4
TOK = 16
HALF = 64
WIDE = 512
CHIP = 1024
FF = 896
GU = 2 * FF
ALL = 3 * FF
MODEL = 4096


def mm(a, b):
    return jnp.dot(a, b, preferred_element_type=F32)


def mm_nt(a, b):
    return lax.dot_general(a, b, (((1,), (1,)), ((), ())), preferred_element_type=F32)


def body(
    tok_ref, cot_ref, gain_ref, gw_ref, uw_ref, dw_ref, gm_ref, um_ref, dm_ref,
    mixed_ref, ig_ref, gg_ref, ug_ref, dg_ref,
    gwb, uwb, dwb, tokn, cotn, xn, gain8, ssq, invn, pulls, totals,
    gath, wgu, wd, part, rel, full, hid, outp, rs1, sum1, rs2,
    acc_gu, acc_d, xt, ht, send_gu, send_d, recv_gu, recv_d,
    l_s, w_s, w_r, p1_r, p2_r, r_s, r_r, f_s, f_r, t_r, g_r, h_r, a_s, a_r, b_r, q_r, gath_s, hid_s, sum_s, line_s,
):
    row = lax.axis_index("row")
    col = lax.axis_index("col")
    z, x, y, c = row // 4, row % 4, col // 2, col % 2
    other = 1 - c
    up, dn, op = (y + 1) % 4, (y + 3) % 4, (y + 2) % 4

    def dev(dz, dx, dy, dc):
        return (dz * 4 + dx, dy * 2 + dc)

    twin = dev(z, x, y, other)
    up_dev, dn_dev = dev(z, x, up, c), dev(z, x, dn, c)

    def zdev(j):
        return dev((z + j) % 4, x, y, c)

    def xdev(j):
        return dev(z, (x + j) % 4, y, c)

    def ydev(j):
        return dev(z, x, (y + j) % 4, c)

    def rc(src, dst, ss, rs, to):
        return pltpu.make_async_remote_copy(
            src_ref=src, dst_ref=dst, send_sem=ss, recv_sem=rs, device_id=to, device_id_type=MESH
        )

    def start(copies):
        for copy in copies:
            copy.start()

    def finish(copies):
        for copy in copies:
            copy.wait()

    def tiles(count):
        across = max(n for n in range(1, 15) if count % n == 0)
        return acc_gu.at[pl.ds(0, 8 * (count // across)), pl.ds(0, 128 * across)]

    def arrive(sem, count):
        rc(tiles(count), tiles(count), sem, sem, twin).wait_recv()

    def leave(sem, count):
        rc(tiles(count), tiles(count), sem, sem, twin).wait_send()

    lo = pl.ds(0, CHIP)
    hi = pl.ds(CHIP, CHIP)

    def strip(a, h):
        return pl.ds(a * CHIP + h * WIDE, WIDE)

    def to_lanes(column):
        n = column.shape[0]
        spot = lax.broadcasted_iota(jnp.int32, (n, 128), 0) == lax.broadcasted_iota(jnp.int32, (n, 128), 1)
        line = jnp.sum(jnp.where(spot, jnp.broadcast_to(column, (n, 128)), 0.0), axis=0, keepdims=True)
        return jnp.broadcast_to(line, (8, 128))

    def to_column(line, n):
        spot = lax.broadcasted_iota(jnp.int32, (n, 128), 0) == lax.broadcasted_iota(jnp.int32, (n, 128), 1)
        return jnp.sum(jnp.where(spot, jnp.broadcast_to(line, (n, 128)), 0.0), axis=1, keepdims=True)

    mine = pl.ds(pl.multiple_of(c * WIDE, WIDE), WIDE)
    theirs = pl.ds(pl.multiple_of(other * WIDE, WIDE), WIDE)
    def width(a):
        return WIDE + 128 * (1 - a)

    def out_strip(a, h):
        return pl.ds(2 * (WIDE + 128) * a + h * width(a), width(a))

    barrier = pltpu.get_barrier_semaphore()
    peers = [twin] + [f(j) for f in (xdev, ydev, zdev) for j in (1, 2, 3)]
    peers += [dev(z, x, (y + j) % 4, other) for j in (1, 2, 3)]
    peers += [dev((z + j) % 4, x, y, other) for j in (1, 2, 3)] + [dev(z, (x + j) % 4, y, other) for j in (1, 2, 3)]
    for peer in peers:
        pl.semaphore_signal(barrier, inc=1, device_id=peer, device_id_type=MESH)

    loads = [
        pltpu.make_async_copy(src, dst, l_s.at[n])
        for n, (src, dst) in enumerate(
            ((cot_ref, cotn), (tok_ref, tokn), (dw_ref, dwb), (gw_ref, gwb), (uw_ref, uwb))
        )
    ]
    start(loads)
    gain8[...] = jnp.broadcast_to(gain_ref[...], (8, WIDE))
    finish(loads[0:3])

    @pl.loop(0, 7)
    def _(i):
        rows = pl.ds(pl.multiple_of(i * 128, 128), 128)
        for j in range(4):
            to = pl.ds(pl.multiple_of(c * WIDE + j * 128, 128), 128)
            keep = dm_ref[j, i].astype(F32)
            wd[rows, to] = (dwb[rows, j * 128 : j * 128 + 128].astype(F32) * keep).astype(BF)

    pl.semaphore_wait(barrier, len(peers))

    own = (xn, cotn)

    def at_strip(a, core):
        return pl.ds(pl.multiple_of(a * CHIP + core * WIDE, WIDE), WIDE)

    def near(k, a):
        def one(core, to):
            rows = pl.ds(pl.multiple_of(core * HALF + k * TOK, TOK), TOK)
            return rc(own[a].at[rows, :], gath.at[k, z, x, :, at_strip(a, c)], gath_s.at[k], p1_r.at[k, a], to)

        far = [
            one(core, dev((z + c * j) % 4, (x + other * j) % 4, y, core)) for j in (1, 2, 3) for core in (0, 1)
        ]
        return far + [one(other, twin)]

    def keep(a):
        for k in range(CHUNKS):
            rows = pl.ds(pl.multiple_of(c * HALF + k * TOK, TOK), TOK)
            gath[k, z, x, :, at_strip(a, c)] = own[a][rows, :]

    def rest(k, a):
        def one(h, to, j):
            block = gath.at[k, z, :, :, strip(a, 0)] if h == 0 else gath.at[k, :, x, :, strip(a, 1)]
            return rc(block, block, gath_s.at[k], p2_r.at[k, a], to(j))

        return [one(h, to, j) for j in (1, 2, 3) for h, to in ((0, zdev), (1, xdev))]

    def near_here(k, a):
        arrive(p1_r.at[k, a], 28)

    def rest_here(k, a):
        arrive(p2_r.at[k, a], 96)

    start(near(0, 1))
    tok = tokn[...].astype(F32)
    ssq[col] = to_lanes(jnp.sum(tok * tok, axis=1, keepdims=True))
    start(
        [
            rc(ssq.at[col], ssq.at[col], line_s.at[0], q_r.at[0], to)
            for to in [twin] + [dev(z, x, (y + j) % 4, core) for j in (1, 2, 3) for core in (0, 1)]
        ]
    )
    exchange = [
        rc(wd.at[:, mine], wd.at[:, mine], w_s.at[0], w_r.at[0], twin),
        rc(wgu.at[mine, :], wgu.at[mine, :], w_s.at[1], w_r.at[1], twin),
        rc(send_gu, recv_gu, w_s.at[2], w_r.at[2], twin),
        rc(send_d, recv_d, w_s.at[3], w_r.at[3], twin),
    ]
    start(exchange[0:1])
    keep(1)
    finish(loads[3:5])

    @pl.loop(0, 4)
    def _(i):
        rows = pl.ds(pl.multiple_of(i * 128, 128), 128)
        to = pl.ds(pl.multiple_of(c * WIDE + i * 128, 128), 128)
        for j in range(7):
            cols = slice(j * 128, j * 128 + 128)
            keep = gm_ref[i, j].astype(F32)
            wgu[to, j * 128 : j * 128 + 128] = (gwb[rows, cols].astype(F32) * keep).astype(BF)
            keep = um_ref[i, j].astype(F32)
            wgu[to, FF + j * 128 : FF + j * 128 + 128] = (uwb[rows, cols].astype(F32) * keep).astype(BF)

    start(exchange[1:2])
    near_here(0, 1)
    start(rest(0, 1))
    arrive(q_r.at[0], 7)
    squares = ssq[0]
    for n in range(1, 8):
        squares += ssq[n]
    inv = 1.0 / jnp.sqrt(to_column(squares[0:1, :], 128) / MODEL + epsilon)
    invn[...] = jnp.broadcast_to(inv, (2 * HALF, 128))
    xn[...] = (tokn[...].astype(F32) * gain8[0:1, :] * inv).astype(BF)
    start(near(0, 0))
    keep(0)

    @pl.loop(0, 16)
    def _(i):
        acc_gu[pl.ds(pl.multiple_of(i * 64, 64), 64), :] = jnp.zeros((64, GU), F32)
        acc_d[pl.ds(pl.multiple_of(i * 56, 56), 56), :] = jnp.zeros((56, CHIP), F32)

    near_here(0, 0)
    start(rest(0, 0))
    start(near(1, 1) + near(1, 0))
    finish(exchange[0:2])

    def span(a):
        return pl.ds(GU, FF) if a == 1 else pl.ds(0, GU)

    def relay(k, s, a):
        one = part.at[s, op, pl.ds(0, 32), span(a)]
        two = part.at[s, op, pl.ds(32, 32), span(a)]
        return [
            rc(one, rel.at[k, 0, :, span(a)], r_s.at[k, a], r_r.at[k, a], up_dev),
            rc(two, rel.at[k, 1, :, span(a)], r_s.at[k, a], r_r.at[k, a], dn_dev),
        ]

    def quarter(k, s, a):
        return [
            rc(part.at[s, up, :, span(a)], full.at[k, 0, :, span(a)], f_s.at[k], f_r.at[k], up_dev),
            rc(part.at[s, dn, :, span(a)], full.at[k, 1, :, span(a)], f_s.at[k], f_r.at[k], dn_dev),
        ]

    def kind(b):
        return pl.ds(FF, GU) if b == 1 else pl.ds(0, FF)

    def share(k, b, later):
        one = hid.at[k, y, pl.ds(32 if later else 0, 32), kind(b)]
        two = hid.at[k, y, pl.ds(0 if later else 32, 32), kind(b)]
        return [
            rc(one, one, hid_s.at[k], g_r.at[k, b, later], up_dev),
            rc(two, two, hid_s.at[k], g_r.at[k, b, later], dn_dev),
        ]

    def pass_on(k, b):
        first = hid.at[k, dn, pl.ds(0, 32), kind(b)]
        second = hid.at[k, up, pl.ds(32, 32), kind(b)]
        return [
            rc(first, first, hid_s.at[k], h_r.at[k, b], up_dev),
            rc(second, second, hid_s.at[k], h_r.at[k, b], dn_dev),
        ]

    def tell(k):
        return [rc(pulls.at[k, y], pulls.at[k, y], line_s.at[0], t_r.at[k], ydev(j)) for j in (1, 2, 3)]

    def scatter(k, s, a):
        def one(h, to, j):
            strip_a = out_strip(a, h)
            block = outp.at[s, :, (x + j) % 4, :, strip_a] if h == 0 else outp.at[s, (z + j) % 4, :, :, strip_a]
            return rc(
                block, rs1.at[k, a, h, j - 1, :, :, pl.ds(0, width(a))],
                a_s.at[k, a], a_r.at[k, a], to(j),
            )

        return [one(h, to, j) for j in (1, 2, 3) for h, to in ((0, xdev), (1, zdev))]

    at_mine = z * other + x * c
    at_theirs = z * c + x * other

    def scatter_rest(k, a):
        def one(h, place, j, to):
            return rc(
                sum1.at[k, a, h, place, :, pl.ds(0, width(a))], rs2.at[k, a, c, j, :, pl.ds(0, width(a))],
                sum_s.at[0], b_r.at[k, a], to,
            )

        far = [
            one(h, ((x if h else z) + j) % 4, j,
                dev(z, (x + j) % 4, y, 1) if h else dev((z + j) % 4, x, y, 0))
            for j in (1, 2, 3) for h in (0, 1)
        ]
        return far + [one(other, at_theirs, 0, twin)]

    def await_rest(k, a):
        arrive(b_r.at[k, a], 28 if a == 1 else 35)

    def project_pre(k):
        s = k % 2

        @pl.loop(0, 7)
        def _(n):
            cols = pl.ds(pl.multiple_of(n * 256, 256), 256)
            got = mm(gath[k, :, :, :, lo].reshape(256, CHIP), wgu[:, cols])
            part[s, :, :, cols] = got.astype(BF).reshape(4, 64, 256)

    def project_back(k):
        s = k % 2
        for n, wide in ((0, 256), (256, 256), (512, 256), (768, 128)):
            got = mm_nt(gath[k, :, :, :, hi].reshape(256, CHIP), wd[n : n + wide, :])
            part[s, :, :, GU + n : GU + n + wide] = got.astype(BF).reshape(4, 64, wide)

    def add_relay(k, a):
        s = k % 2
        base, count = (GU, 7) if a == 1 else (0, 14)

        @pl.loop(0, count)
        def _(n):
            cols = pl.ds(pl.multiple_of(base + n * 128, 128), 128)
            part[s, up, 0:32, cols] = (part[s, up, 0:32, cols].astype(F32) + rel[k, 0, :, cols].astype(F32)).astype(BF)
            part[s, dn, 32:64, cols] = (part[s, dn, 32:64, cols].astype(F32) + rel[k, 1, :, cols].astype(F32)).astype(BF)

    def activate(k):
        s = k % 2

        def one(n, pulled):
            def total(base):
                cols = pl.ds(pl.multiple_of(base + n * 128, 128), 128)
                return part[s, y, :, cols].astype(F32) + full[k, 0, :, cols].astype(F32) + full[k, 1, :, cols].astype(F32)

            gate, up_value, back = total(0), total(FF), total(GU)
            sigma = jax.nn.sigmoid(gate)
            activ = gate * sigma
            d_gate = back * up_value * sigma * (1.0 + gate * (1.0 - sigma))
            d_up = back * activ
            hid[k, y, :, pl.ds(pl.multiple_of(n * 128, 128), 128)] = (activ * up_value).astype(BF)
            hid[k, y, :, pl.ds(pl.multiple_of(FF + n * 128, 128), 128)] = d_gate.astype(BF)
            hid[k, y, :, pl.ds(pl.multiple_of(GU + n * 128, 128), 128)] = d_up.astype(BF)
            return pulled + (d_gate * gate + d_up * up_value)

        pulled = lax.fori_loop(0, 7, one, jnp.zeros((HALF, 128), F32))
        pulls[k, y] = to_lanes(jnp.sum(pulled, axis=1, keepdims=True))

    def products_back(k):
        s = k % 2

        @pl.loop(0, 4)
        def _(n):
            cols = pl.ds(pl.multiple_of(n * 256, 256), 256)
            got = mm_nt(hid[k, :, :, FF:ALL].reshape(256, GU), wgu[cols, :])
            outp[s, :, :, :, pl.ds(pl.multiple_of(2 * (WIDE + 128) + n * 256, 256), 256)] = got.astype(BF).reshape(4, 4, TOK, 256)

    def products_out(k):
        s = k % 2

        @pl.loop(0, 4)
        def _(n):
            cols = pl.ds(pl.multiple_of(n * 256, 256), 256)
            got = mm(hid[k, :, :, 0:FF].reshape(256, FF), wd[:, cols])
            to = pl.ds(pl.multiple_of(n * 256 + (n // 2) * 128, 128), 256)
            outp[s, :, :, :, to] = got.astype(BF).reshape(4, 4, TOK, 256)

        for i in range(4):
            pulled = jnp.broadcast_to(to_column(pulls[k, i, 0:1, :], HALF), (HALF, 128)).astype(BF).reshape(4, TOK, 128)
            outp[s, i, :, :, WIDE : WIDE + 128] = pulled
            outp[s, i, :, :, 2 * WIDE + 128 : 2 * WIDE + 256] = pulled

    def sums_gu(k):
        xt[...] = gath[k, :, :, :, lo].reshape(256, CHIP).T

        @pl.loop(0, 7)
        def _(n):
            cols = pl.ds(pl.multiple_of(n * 256, 256), 256)
            from_cols = pl.ds(pl.multiple_of(FF + n * 256, 128), 256)
            pulled = hid[k, :, :, from_cols].reshape(256, 256)
            for m in range(4):
                acc_gu[m * 256 : m * 256 + 256, cols] += mm(xt[m * 256 : m * 256 + 256, :], pulled)

    def sums_d(k):
        ht[...] = hid[k, :, :, 0:FF].reshape(256, FF).T

        @pl.loop(0, 4)
        def _(n):
            cols = pl.ds(pl.multiple_of(n * 256, 256), 256)
            from_cols = pl.ds(pl.multiple_of(CHIP + n * 256, 256), 256)
            cots = gath[k, :, :, :, from_cols].reshape(256, 256)
            for m, high in ((0, 256), (256, 256), (512, 256), (768, 128)):
                acc_d[m : m + high, cols] += mm(ht[m : m + high, :], cots)

    def sum_first(k, a):
        s = k % 2
        for i in range(4):
            for h in range(2):
                total = (outp[s, i, x, :, out_strip(a, 0)] if h == 0 else outp[s, z, i, :, out_strip(a, 1)]).astype(F32)
                for j in range(3):
                    total += rs1[k, a, h, j, i, :, 0 : width(a)].astype(F32)
                sum1[k, a, h, i, :, 0 : width(a)] = total.astype(BF)

    def sum_last(k, a):
        for core, first in ((c, sum1[k, a, c, at_mine, :, 0 : width(a)]), (other, rs2[k, a, other, 0, :, 0 : width(a)])):
            rows = pl.ds(pl.multiple_of(core * HALF + k * TOK, TOK), TOK)
            total = first.astype(F32)
            for j in (1, 2, 3):
                total += rs2[k, a, core, j, :, 0 : width(a)].astype(F32)
            if a == 0:
                mixed_ref[rows, :] = (tokn[rows, :].astype(F32) + total[:, 0:WIDE]).astype(BF)
                totals[rows, :] = total[:, WIDE:]
            else:
                inv = invn[rows, 0:1]
                fix = inv * inv * totals[rows, 0:1] / MODEL
                ig_ref[rows, :] = (
                    cotn[rows, :].astype(F32) + gain8[0:1, :] * (inv * total) - tokn[rows, :].astype(F32) * fix
                ).astype(BF)

    def step(i, carry):
        def at(k):
            return jnp.logical_and(k >= 0, k < CHUNKS)

        @pl.when(at(i - 2))
        def _():
            k = i - 2
            leave(f_s.at[k], 168)
            arrive(f_r.at[k], 168)
            activate(k)
            start(tell(k))
            for b in (0, 1):
                start(share(k, b, 0) + share(k, b, 1))

        @pl.when(at(i - 1))
        def _():
            k = i - 1
            for a in (1, 0):
                leave(r_s.at[k, a], 28 if a == 1 else 56)
                arrive(r_r.at[k, a], 28 if a == 1 else 56)
                add_relay(k, a)
                start(quarter(k, k % 2, a))

        @pl.when(i < CHUNKS)
        def _():
            rest_here(i, 1)
            project_back(i)
            start(relay(i, i % 2, 1))
            rest_here(i, 0)
            project_pre(i)
            start(relay(i, i % 2, 0))

        @pl.when(i + 1 < CHUNKS)
        def _():
            for a in (1, 0):
                near_here(i + 1, a)
                start(rest(i + 1, a))

        @pl.when(i + 2 < CHUNKS)
        def _():
            start(near(i + 2, 1) + near(i + 2, 0))

        @pl.when(at(i - 4))
        def _():
            k = i - 4
            for a in (0, 1):
                leave(a_s.at[k, a], 96 if a == 1 else 120)
                arrive(a_r.at[k, a], 96 if a == 1 else 120)
                sum_first(k, a)
                start(scatter_rest(k, a))

        @pl.when(at(i - 3))
        def _():
            k = i - 3
            arrive(t_r.at[k], 3)
            arrive(g_r.at[k, 0, 1], 28)
            arrive(h_r.at[k, 0], 28)
            products_out(k)
            start(scatter(k, k % 2, 0))
            sums_d(k)

        @pl.when(i - 3 == CHUNKS - 1)
        def _():
            send_d[...] = acc_d[:, theirs].astype(BF)
            start(exchange[3:4])

        @pl.when(at(i - 3))
        def _():
            k = i - 3
            arrive(g_r.at[k, 1, 1], 56)
            arrive(h_r.at[k, 1], 56)
            products_back(k)
            start(scatter(k, k % 2, 1))
            sums_gu(k)

        @pl.when(i - 3 == CHUNKS - 1)
        def _():
            @pl.loop(0, 4)
            def _(n):
                rows = pl.ds(pl.multiple_of(n * 128, 128), 128)
                src = pl.ds(pl.multiple_of(other * WIDE + n * 128, 128), 128)
                send_gu[rows, :] = acc_gu[src, :].astype(BF)

            start(exchange[2:3])

        @pl.when(at(i - 5))
        def _():
            for a in (0, 1):
                await_rest(i - 5, a)
                sum_last(i - 5, a)

        @pl.when(at(i - 2))
        def _():
            for b in (0, 1):
                arrive(g_r.at[i - 2, b, 0], 28 * (1 + b))
                start(pass_on(i - 2, b))

        return carry

    lax.fori_loop(0, CHUNKS + 4, step, 0)

    await_rest(CHUNKS - 1, 0)
    sum_last(CHUNKS - 1, 0)
    finish(exchange[2:4])

    @pl.loop(0, 4)
    def _(i):
        rows = pl.ds(pl.multiple_of(i * 128, 128), 128)
        src = pl.ds(pl.multiple_of(c * WIDE + i * 128, 128), 128)
        for j in range(7):
            cols = slice(j * 128, j * 128 + 128)
            wide = slice(FF + j * 128, FF + j * 128 + 128)
            total = acc_gu[src, cols] + recv_gu[rows, cols].astype(F32)
            gg_ref[rows, cols] = (total * gm_ref[i, j].astype(F32)).astype(BF)
            total = acc_gu[src, wide] + recv_gu[rows, wide].astype(F32)
            ug_ref[rows, cols] = (total * um_ref[i, j].astype(F32)).astype(BF)

    @pl.loop(0, 7)
    def _(i):
        rows = pl.ds(pl.multiple_of(i * 128, 128), 128)
        for j in range(4):
            cols = slice(j * 128, j * 128 + 128)
            src = pl.ds(pl.multiple_of(c * WIDE + j * 128, 128), 128)
            total = acc_d[rows, src] + recv_d[rows, cols].astype(F32)
            dg_ref[rows, cols] = (total * dm_ref[j, i].astype(F32)).astype(BF)

    await_rest(CHUNKS - 1, 1)
    sum_last(CHUNKS - 1, 1)
    for k in range(CHUNKS):
        leave(gath_s.at[k], 2 * (28 + 96))
        leave(hid_s.at[k], 3 * (28 + 56))
    leave(sum_s.at[0], CHUNKS * (28 + 35))
    leave(line_s.at[0], 7 + CHUNKS * 3)


def store(*refs):
    copies = [pltpu.make_async_copy(refs[i], refs[5 + i], refs[10].at[i]) for i in range(5)]
    for copy in copies:
        copy.start()
    for copy in copies:
        copy.wait()


def shards(tokens, cotangent, norm_gain, gate_w, up_w, down_w, gate_b, up_b, down_b):
    vmem = pl.BlockSpec(memory_space=pltpu.VMEM)
    smem = pl.BlockSpec(memory_space=pltpu.SMEM)
    hbm = pl.BlockSpec(memory_space=pltpu.HBM)

    def dma(*shape):
        return pltpu.SemaphoreType.DMA(shape)

    V = pltpu.VMEM
    results = pl.pallas_call(
        body,
        out_shape=(
            V(tokens.shape, BF),
            V(tokens.shape, BF),
            V(gate_w.shape, BF),
            V(up_w.shape, BF),
            V(down_w.shape, BF),
        ),
        in_specs=[hbm, hbm, vmem, hbm, hbm, hbm] + [smem] * 3,
        out_specs=(vmem,) * 5,
        scratch_shapes=[
            V((WIDE, FF), BF),
            V((WIDE, FF), BF),
            V((FF, WIDE), BF),
            V((2 * HALF, WIDE), BF),
            V((2 * HALF, WIDE), BF),
            V((2 * HALF, WIDE), BF),
            V((8, WIDE), F32),
            V((8, 8, 128), F32),
            V((2 * HALF, 128), F32),
            V((CHUNKS, 4, 8, 128), F32),
            V((2 * HALF, 128), F32),
            V((CHUNKS, 4, 4, TOK, 2 * CHIP), BF),
            V((CHIP, GU), BF),
            V((FF, CHIP), BF),
            V((2, 4, 64, ALL), BF),
            V((CHUNKS, 2, 32, ALL), BF),
            V((CHUNKS, 2, 64, ALL), BF),
            V((CHUNKS, 4, 64, ALL), BF),
            V((2, 4, 4, TOK, 2 * (WIDE + 128) + CHIP), BF),
            V((CHUNKS, 2, 2, 3, 4, TOK, WIDE + 128), BF),
            V((CHUNKS, 2, 2, 4, TOK, WIDE + 128), BF),
            V((CHUNKS, 2, 2, 4, TOK, WIDE + 128), BF),
            V((CHIP, GU), F32),
            V((FF, CHIP), F32),
            V((CHIP, 256), BF),
            V((FF, 256), BF),
            V((WIDE, GU), BF),
            V((FF, WIDE), BF),
            V((WIDE, GU), BF),
            V((FF, WIDE), BF),
            dma(5),
            dma(4),
            dma(4),
            dma(CHUNKS, 2),
            dma(CHUNKS, 2),
            dma(CHUNKS, 2),
            dma(CHUNKS, 2),
            dma(CHUNKS),
            dma(CHUNKS),
            dma(CHUNKS),
            dma(CHUNKS, 2, 2),
            dma(CHUNKS, 2),
            dma(CHUNKS, 2),
            dma(CHUNKS, 2),
            dma(CHUNKS, 2),
            dma(1),
            dma(CHUNKS),
            dma(CHUNKS),
            dma(1),
            dma(1),
        ],
        compiler_params=pltpu.CompilerParams(
            collective_id=0, has_side_effects=True, vmem_limit_bytes=56 * 1024 * 1024
        ),
        cost_estimate=pl.CostEstimate(flops=17_000_000_000, bytes_accessed=6_000_000, transcendentals=2_000_000),
        name="ffn",
    )(tokens, cotangent, norm_gain.reshape(1, -1), gate_w, up_w, down_w, gate_b, up_b, down_b.T)
    return pl.pallas_call(
        store,
        out_shape=tuple(jax.ShapeDtypeStruct(r.shape, r.dtype) for r in results),
        in_specs=[vmem] * 5,
        out_specs=(pl.BlockSpec(memory_space=pl.ANY),) * 5,
        scratch_shapes=[pltpu.SemaphoreType.DMA((5,))],
        name="store",
    )(*[pltpu.with_memory_space_constraint(r, pltpu.VMEM) for r in results])


def solution(mesh):
    in_specs = (
        P("row", "col"),
        P("row", "col"),
        P("col"),
        P("col", "row"),
        P("col", "row"),
        P("row", "col"),
        P("col", "row"),
        P("col", "row"),
        P("row", "col"),
    )
    out_specs = (
        P("row", "col"),
        P("row", "col"),
        P("col", "row"),
        P("col", "row"),
        P("row", "col"),
    )
    return jax.shard_map(shards, mesh=mesh, in_specs=in_specs, out_specs=out_specs, check_vma=False)
```
